128 devices in a mesh: dp: 8 (over y, core), seq: 16 (over x, z).
Axes of the slice: x: 4, y: 4, z: 4, core: 2. Of those that a mesh axis runs over, the one named last changes fastest.
Arguments:
- queries: bfloat16 [8, 6144, 2048], P('dp', 'seq'), may hold values from -256 to 256
- database: bfloat16 [64, 128, 896], P('seq'), may hold values from -6 to 6
- kv_weight: bfloat16 [896, 4096], replicated, may hold values from -1 to 1
- neighbours: int32 [8, 96, 2], P('dp', 'seq'), may hold values from 0 to 63, as said below
- out_grad: bfloat16 [8, 6144, 2048], P('dp', 'seq'), may hold values from -12 to 12
Outputs:
- attended: bfloat16 [8, 6144, 2048], P('dp', 'seq')
- query_grad: bfloat16 [8, 6144, 2048], P('dp', 'seq')
- row_grad: float32 [64, 128, 896], P('seq', 'dp')
The draws below stay inside these ranges and needn't reach their ends.
Inputs may be any that keep to these rules, and one draw needn't show every extreme that they name: `neighbours`: neighbour n is held by index n // 4 of seq. The two ids of a group differ. Among the ids of groups s * 6 - 1 to s * 6 + 4 of one sequence (groups from 0 on), at most 2 are held by one index of seq, and in each such set at least one index is named exactly 2 times; in one of the sequences such an index is the same for every s.
All inputs are finite; a program needn't handle non-finite values.
Results may differ from the reference program's by a relative error of at most 0.02.
The reference program's roundings to bfloat16 on the way count: a program that leaves them out, or rounds other values in their place, can miss the bound.
Values may be sent and summed in bfloat16 or wider, within the bound.
No kernel may reach another device: no remote copies, remote signals or barrier semaphores. Data moves between devices by JAX's collectives and lax.ppermute only.
A program may use at most 192 MiB of HBM per device.

```python
import jax
import jax.numpy as jnp
from jax import lax

HEADS = 16
HD = 128
ENC = 896
GROUP = 64
NTOK = 128
C_DEV = 6
NBS = 4
HH = 2048
SEQS = 8
NCH = 96
LEN = 6144
NB = 64
N_DP = 8
N_SEQ = 16


def neighbour_ids(key):
    base = jax.random.fold_in(key, 101)
    subkeys = jax.random.split(base, 10)
    ref_total = 2 * C_DEV
    capacity = max(2, (ref_total + N_SEQ - 1) // N_SEQ)
    windows = N_DP * N_SEQ
    hot_sequence = jax.random.randint(subkeys[0], (), 0, N_DP)
    hot_holder = jax.random.randint(subkeys[1], (), 0, N_SEQ)
    window_hot = jax.random.randint(subkeys[2], (N_DP, N_SEQ), 0, N_SEQ)
    sequence_index = jnp.arange(N_DP)[:, None]
    hot = jnp.where(sequence_index == hot_sequence, hot_holder, window_hot).reshape(windows)
    pool_size = (N_SEQ - 1) * capacity
    shuffled = jax.vmap(lambda sub: jax.random.permutation(sub, pool_size))(jax.random.split(subkeys[3], windows))
    others = shuffled[:, :ref_total - capacity] // capacity
    others = others + (others >= hot[:, None]).astype(jnp.int32)
    in_order = jnp.concatenate([jnp.broadcast_to(hot[:, None], (windows, capacity)), others], axis=1)
    order_keys = jax.vmap(lambda sub: jax.random.permutation(sub, ref_total))(jax.random.split(subkeys[4], windows))
    first_window = (jnp.arange(windows) % N_SEQ == 0)[:, None]
    early = (jnp.arange(ref_total) < 2)[None, :]
    order_keys = order_keys + jnp.where(first_window & early, ref_total, 0)
    order = jnp.argsort(order_keys, axis=1)
    position_rank = jnp.argsort(order, axis=1)
    holders = jnp.take_along_axis(in_order, position_rank, axis=1).reshape(windows, C_DEV, 2)
    first_local = jax.random.randint(subkeys[5], (windows, C_DEV), 0, NBS)
    step_local = jax.random.randint(subkeys[6], (windows, C_DEV), 1, NBS)
    other_local = jax.random.randint(subkeys[7], (windows, C_DEV), 0, NBS)
    second_local = jnp.where(holders[:, :, 0] == holders[:, :, 1], (first_local + step_local) % NBS, other_local)
    ids = holders * NBS + jnp.stack([first_local, second_local], axis=-1)
    ids = ids.reshape(N_DP, N_SEQ * C_DEV, 2)
    last_first = jax.random.randint(subkeys[8], (N_DP, 1), 0, NBS * N_SEQ)
    last_step = jax.random.randint(subkeys[9], (N_DP, 1), 1, NBS * N_SEQ)
    last_ids = jnp.stack([last_first, (last_first + last_step) % (NBS * N_SEQ)], axis=-1)
    return jnp.concatenate([ids[:, 1:], last_ids], axis=1).astype(jnp.int32)


def encoder_values(key):
    sub = jax.random.fold_in(key, 102)
    shape = (NBS * N_SEQ, NTOK, ENC)
    return jnp.clip(jax.random.normal(sub, shape, jnp.float32), -6.0, 6.0)


def weight_values(key):
    sub = jax.random.fold_in(key, 104)
    shape = (ENC, 2 * HEADS * HD)
    spread = ENC ** (-0.5)
    limit = min(6.0 * spread, 1.0)
    drawn = jax.random.normal(sub, shape, jnp.float32) * spread
    return jnp.clip(drawn, -limit, limit)


def draw_queries(key, part):
    sub = jax.random.fold_in(key, 103)
    shape = (N_DP, C_DEV * GROUP * N_SEQ, HEADS * HD)
    drawn = 1.5 * jnp.clip(jax.random.normal(sub, shape, jnp.float32), -6.0, 6.0)
    return jnp.clip(drawn, -256.0, 256.0).astype(jnp.bfloat16)


def draw_database(key, part):
    return encoder_values(key).astype(jnp.bfloat16)


def draw_kv_weight(key, part):
    return weight_values(key).astype(jnp.bfloat16)


def draw_neighbours(key, part):
    return neighbour_ids(key)


def level_of(own_key, shape, cuts, smallest, largest):
    loudness, own = 1.0, jax.random.fold_in(own_key, 6)
    for dim, shards_of in cuts:
        draws = jnp.exp(jax.random.uniform(jax.random.fold_in(own, dim), (shards_of,), jnp.float32, smallest / len(cuts), largest / len(cuts)))
        loudness = loudness * jnp.repeat(draws, shape[dim] // shards_of).reshape([-1 if axis == dim else 1 for axis in range(len(shape))])
    return loudness


def scatter_about(key, extent, scale, most, shards=(), kind=jnp.bfloat16):
    values = scale * jax.random.normal(key, extent, jnp.float32)
    if shards:
        values = values * level_of(key, extent, shards, -0.22, 0.18)
    return jnp.clip(values, -most, most).astype(kind)


def setup_inputs(seed: int = 0) -> dict:
    key_list = jax.random.split(jax.random.key(seed), 6)
    queries = draw_queries(jax.random.fold_in(key_list[5], 71), 0)
    database = draw_database(jax.random.fold_in(key_list[5], 71), 0)
    kv_weight = draw_kv_weight(jax.random.fold_in(key_list[5], 71), 0)
    neighbours = draw_neighbours(jax.random.fold_in(key_list[5], 71), 0)
    out_grad = scatter_about(key_list[4], (SEQS, LEN, HH), 2.0, 12.0, ((0, 8), (1, 16)))
    return dict(queries=queries, database=database, kv_weight=kv_weight, neighbours=neighbours, out_grad=out_grad)


def reference(queries, database, kv_weight, neighbours, out_grad):
    scale = HD ** -0.5
    attn_width = HEADS * HD
    flat_rows = database.reshape(NB * NTOK, ENC)
    projected = jnp.dot(flat_rows, kv_weight, preferred_element_type=jnp.float32).astype(jnp.bfloat16)
    projected = projected.reshape(NB, NTOK, 2, HEADS, HD)
    earlier_ids = jnp.concatenate([neighbours[:, :1], neighbours[:, :-1]], axis=1).astype(jnp.int32)
    group_live = jnp.arange(NCH) > 0

    def one_sequence(inputs):
        query_seq, id_seq, grad_seq = inputs
        gathered = projected[id_seq].reshape(NCH, 2 * NTOK, 2, HEADS, HD)
        key_blocks = gathered[:, :, 0].astype(jnp.float32)
        value_blocks = gathered[:, :, 1].astype(jnp.float32)
        query_blocks = query_seq.reshape(NCH, GROUP, HEADS, HD).astype(jnp.float32)
        scores = jnp.einsum("cqhd,ckhd->chqk", query_blocks, key_blocks) * scale
        top_score = jnp.max(scores, axis=-1, keepdims=True)
        raised = jnp.exp(scores - top_score)
        weights_soft = raised / jnp.sum(raised, axis=-1, keepdims=True)
        weights_half = weights_soft.astype(jnp.bfloat16).astype(jnp.float32)
        attended = jnp.einsum("chqk,ckhd->cqhd", weights_half, value_blocks)
        attended = jnp.where(group_live[:, None, None, None], attended, 0.0).astype(jnp.bfloat16)
        grad_blocks = grad_seq.reshape(NCH, GROUP, HEADS, HD)
        grad_blocks = jnp.where(group_live[:, None, None, None], grad_blocks, jnp.zeros((), jnp.bfloat16)).astype(jnp.float32)
        grad_weights = jnp.einsum("cqhd,ckhd->chqk", grad_blocks, value_blocks)
        value_grad = jnp.einsum("chqk,cqhd->ckhd", weights_half, grad_blocks)
        row_dot = jnp.sum(weights_soft * grad_weights, axis=-1, keepdims=True)
        score_grad = (weights_soft * (grad_weights - row_dot)).astype(jnp.bfloat16).astype(jnp.float32)
        query_grad = (jnp.einsum("chqk,ckhd->cqhd", score_grad, key_blocks) * scale).astype(jnp.bfloat16)
        key_grad = jnp.einsum("chqk,cqhd->ckhd", score_grad, query_blocks) * scale
        both_grad = jnp.stack([key_grad, value_grad], axis=2).astype(jnp.bfloat16)
        both_grad = both_grad.reshape(NCH * 2 * NTOK, 2 * attn_width)
        row_terms = jnp.dot(both_grad, kv_weight.T, preferred_element_type=jnp.float32).astype(jnp.bfloat16)
        row_terms = row_terms.reshape(NCH * 2, NTOK, ENC).astype(jnp.float32)
        summed = jax.ops.segment_sum(row_terms, id_seq.reshape(NCH * 2), num_segments=NB)
        return attended.reshape(LEN, attn_width), query_grad.reshape(LEN, attn_width), summed

    attended, query_grad, summed = lax.map(one_sequence, (queries, earlier_ids, out_grad))
    return attended, query_grad, jnp.sum(summed, axis=0)
```

```python
import functools

import jax
import jax.numpy as jnp
from jax import lax
from jax.experimental import pallas as pl
from jax.experimental.pallas import tpu as pltpu
from jax.sharding import Mesh
from jax.sharding import PartitionSpec as P

HD = 128
GROUP = 64
SEQ = ("x", "z")
DP = ("y", "c")
LINE = ("y", "c", "x")
CHUNKS = 2
HEAD_BATCH = 8
F32 = jnp.float32
BF16 = jnp.bfloat16


def dot(a, b, ca, cb):
    return lax.dot_general(a, b, (((ca,), (cb,)), ((), ())), preferred_element_type=F32)


def pack_kernel(first_group, group_count, chunk_groups, ids_ref, table_ref, out_ref):
    def per_dest(dest, carry):
        for g in range(chunk_groups):
            at = dest * 2 * group_count + 2 * (first_group + g)
            first, second = ids_ref[at], ids_ref[at + 1]
            a = table_ref[first >> 2, first & 3].astype(F32)
            b = table_ref[second >> 2, second & 3].astype(F32)
            out_ref[dest, g] = jnp.concatenate([a[:4], b[:4], a[4:], b[4:]], axis=0).astype(BF16)
        return carry

    lax.fori_loop(0, out_ref.shape[0], per_dest, 0)


def pack(ids, table, first_group, group_count, chunk_groups):
    dests, enc = table.shape[0], table.shape[-1]
    return pl.pallas_call(
        functools.partial(pack_kernel, first_group, group_count, chunk_groups),
        out_shape=jax.ShapeDtypeStruct((dests, chunk_groups, 16, enc), BF16),
        in_specs=[
            pl.BlockSpec(memory_space=pltpu.SMEM),
            pl.BlockSpec(memory_space=pltpu.VMEM),
        ],
        out_specs=pl.BlockSpec(memory_space=pltpu.VMEM),
        compiler_params=pltpu.CompilerParams(vmem_limit_bytes=16 << 20),
        name="pack",
    )(ids, table)


def attend_kernel(
    heads, first_group, live_ref, rows_ref, w_ref, q_ref, g_ref, *rest
):
    att_ref, qg_ref, term_ref, kv, kv_grad, q_turned, g_turned = rest[-7:]
    scale = HD**-0.5
    width = heads * HD
    live = (live_ref[0] > 0) | (pl.program_id(0) + first_group > 0)
    rows = rows_ref[...].reshape(-1, rows_ref.shape[-1])
    kv[...] = dot(rows, w_ref[...], 1, 0).astype(BF16)
    grads = jnp.where(live, g_ref[...], jnp.zeros((), BF16))
    q_turned[...] = jnp.transpose(q_ref[...])
    g_turned[...] = jnp.transpose(grads)
    for base in range(0, heads, HEAD_BATCH):
        keys = [slice(h * HD, (h + 1) * HD) for h in range(base, base + HEAD_BATCH)]
        values = [slice(width + h * HD, width + (h + 1) * HD) for h in range(base, base + HEAD_BATCH)]
        scores = [dot(q_ref[:, k], kv[:, k], 1, 1) * scale for k in keys]
        grad_probs = [dot(grads[:, k], kv[:, v], 1, 1) for k, v in zip(keys, values)]
        raised = [jnp.exp(s - jnp.max(s, axis=-1, keepdims=True)) for s in scores]
        probs = [e / jnp.sum(e, axis=-1, keepdims=True) for e in raised]
        halves = [p.astype(BF16) for p in probs]
        score_grads = [
            (p * (gp - jnp.sum(p * gp, axis=-1, keepdims=True))).astype(BF16)
            for p, gp in zip(probs, grad_probs)
        ]
        for k, v, half, sg in zip(keys, values, halves, score_grads):
            att_ref[:, k] = jnp.where(live, dot(half, kv[:, v], 1, 0), 0.0).astype(BF16)
            qg_ref[:, k] = (dot(sg, kv[:, k], 1, 0) * scale).astype(BF16)
            kv_grad[k, :] = (dot(q_turned[k, :], sg, 1, 0) * scale).astype(BF16)
            kv_grad[v, :] = dot(g_turned[k, :], half, 1, 0).astype(BF16)
    terms = jnp.transpose(dot(w_ref[...], kv_grad[...], 1, 0)).astype(BF16)
    term_ref[...] = terms.reshape(term_ref.shape)


def attend(live, rows, weight, queries, grads, before, first_group, line):
    slices, chunk_groups, _, enc = rows.shape
    tokens, width = queries.shape
    keys = slices * 16
    block = pl.BlockSpec((GROUP, width), lambda i, l: (i + first_group, 0))
    flops = chunk_groups * (2 * 2 * keys * enc * 2 * width + 6 * 2 * GROUP * keys * width)
    return pl.pallas_call(
        functools.partial(attend_kernel, width // HD, first_group),
        out_shape=[
            jax.ShapeDtypeStruct((tokens, width), BF16),
            jax.ShapeDtypeStruct((tokens, width), BF16),
            jax.ShapeDtypeStruct((line, chunk_groups, keys // line, enc), BF16),
        ],
        grid_spec=pltpu.PrefetchScalarGridSpec(
            num_scalar_prefetch=1,
            grid=(chunk_groups,),
            in_specs=[
                pl.BlockSpec((slices, 1, 16, enc), lambda i, l: (0, i, 0, 0)),
                pl.BlockSpec((enc, 2 * width), lambda i, l: (0, 0)),
                block,
                block,
            ]
            + [pl.BlockSpec(memory_space=pl.ANY)] * len(before),
            out_specs=[
                block,
                block,
                pl.BlockSpec((line, 1, keys // line, enc), lambda i, l: (0, i, 0, 0)),
            ],
            scratch_shapes=[
                pltpu.VMEM((keys, 2 * width), BF16),
                pltpu.VMEM((2 * width, keys), BF16),
                pltpu.VMEM((width, GROUP), BF16),
                pltpu.VMEM((width, GROUP), BF16),
            ],
        ),
        input_output_aliases={5 + n: n for n in range(len(before))},
        cost_estimate=pl.CostEstimate(
            flops=flops, bytes_accessed=16 << 20, transcendentals=0
        ),
        compiler_params=pltpu.CompilerParams(vmem_limit_bytes=44 << 20),
        name="attend",
    )(live, rows, weight, queries, grads, *before)


def exchange(block, axes):
    return lax.all_to_all(block, axes, split_axis=0, concat_axis=0, tiled=True)


def body(queries, database, kv_weight, neighbours, out_grad):
    seq_count = lax.axis_size(SEQ)
    seq_index = lax.axis_index(SEQ)
    x_count, z_count = lax.axis_size("x"), lax.axis_size("z")
    dp_count = lax.axis_size(DP)
    line = lax.axis_size(LINE)
    group_count = neighbours.shape[1]
    ref_count = 2 * group_count
    held, row_tokens, enc = database.shape
    width = queries.shape[2]
    chunk_groups = group_count // CHUNKS
    own_tokens = row_tokens // line

    slices = database.reshape(held, seq_count, row_tokens // seq_count, enc).transpose(1, 0, 2, 3)
    id_rows = jnp.pad(
        neighbours.reshape(1, ref_count).astype(BF16), ((0, row_tokens // seq_count - 1), (0, enc - ref_count))
    )
    id_rows = jnp.broadcast_to(id_rows[None, None], (seq_count, 1) + id_rows.shape)
    table = exchange(jnp.concatenate([slices, id_rows], axis=1), SEQ)
    all_ids = table[:, held, 0, :ref_count].astype(jnp.int32).reshape(-1)
    windows = jnp.concatenate([all_ids[:2], all_ids[:-2]])

    live = (seq_index > 0).astype(jnp.int32).reshape(1)
    rows = [
        exchange(pack(windows, table, c * chunk_groups, group_count, chunk_groups), SEQ)
        for c in range(CHUNKS)
    ]

    z_index = lax.axis_index("z")
    column = lax.dynamic_index_in_dim(
        windows.reshape(x_count, z_count, ref_count), z_index, axis=1, keepdims=False
    )
    column_live = (
        (jnp.arange(x_count)[:, None] > 0) | (z_index > 0) | (jnp.arange(ref_count)[None, :] >= 2)
    )
    column = jnp.where(column_live, column, -1)
    line_ids = lax.all_gather(column, DP, axis=0, tiled=False).reshape(line, group_count, 2)
    keys = jnp.where(
        line_ids[..., None] >= 0, line_ids[..., None] * own_tokens + jnp.arange(own_tokens), -1
    )

    done = ()
    total = jnp.zeros((seq_count * held * own_tokens, enc), F32)
    for c in range(CHUNKS):
        *done, terms = attend(
            live, rows[c], kv_weight, queries[0], out_grad[0], done, c * chunk_groups, line
        )
        back = exchange(terms, LINE)
        chunk_keys = keys[:, c * chunk_groups : (c + 1) * chunk_groups].reshape(1, -1)
        match = (jnp.arange(total.shape[0])[:, None] == chunk_keys).astype(BF16)
        total = total + jnp.dot(match, back.reshape(-1, enc), preferred_element_type=F32)
    owned = exchange(total.astype(BF16).reshape(seq_count, held * own_tokens, enc), SEQ)
    owned = owned.reshape(x_count, z_count, held, own_tokens, enc).astype(F32).sum(axis=1)
    row_grad = owned.transpose(1, 0, 2, 3).reshape(held, x_count * own_tokens, enc)
    return done[0][None], done[1][None], row_grad


def solution(mesh):
    split = Mesh(mesh.devices.reshape(4, 2, 4, 4), ("y", "c", "x", "z"))
    return jax.shard_map(
        body,
        mesh=split,
        in_specs=(
            P(DP, SEQ, None),
            P(SEQ, None, None),
            P(),
            P(DP, SEQ, None),
            P(DP, SEQ, None),
        ),
        out_specs=(P(DP, SEQ, None), P(DP, SEQ, None), P(SEQ, DP, None)),
        check_vma=False,
    )
```

```python
import functools

import jax
import jax.numpy as jnp
from jax import lax
from jax.experimental import pallas as pl
from jax.experimental.pallas import tpu as pltpu
from jax.sharding import Mesh
from jax.sharding import PartitionSpec as P

HD = 128
GROUP = 64
SEQ = ("x", "z")
DP = ("y", "c")
LINE = ("y", "c", "x")
CHUNKS = 2
HEAD_BATCH = 4
LANES = 128
F32 = jnp.float32
BF16 = jnp.bfloat16


def dot(a, b, ca, cb):
    return lax.dot_general(a, b, (((ca,), (cb,)), ((), ())), preferred_element_type=F32)


def pack_kernel(first_group, group_count, chunk_groups, lane_tiles, ids_ref, table_ref, out_ref):
    def per_dest(dest, carry):
        for g in range(chunk_groups):
            at = dest * 2 * group_count + 2 * (first_group + g)
            first, second = ids_ref[at], ids_ref[at + 1]
            for t in range(lane_tiles):
                a = table_ref[first >> 2, (first & 3) * lane_tiles + t].astype(F32)
                b = table_ref[second >> 2, (second & 3) * lane_tiles + t].astype(F32)
                out_ref[dest, g, :, t * LANES : (t + 1) * LANES] = jnp.concatenate(
                    [a[:4], b[:4], a[4:], b[4:]], axis=0
                ).astype(BF16)
        return carry

    lax.fori_loop(0, out_ref.shape[0], per_dest, 0)


def pack(ids, table, enc, first_group, group_count, chunk_groups):
    dests = table.shape[0]
    return pl.pallas_call(
        functools.partial(pack_kernel, first_group, group_count, chunk_groups, enc // LANES),
        out_shape=jax.ShapeDtypeStruct((dests, chunk_groups, 16, enc), BF16),
        in_specs=[
            pl.BlockSpec(memory_space=pltpu.SMEM),
            pl.BlockSpec(memory_space=pltpu.VMEM),
        ],
        out_specs=pl.BlockSpec(memory_space=pltpu.VMEM),
        compiler_params=pltpu.CompilerParams(vmem_limit_bytes=16 << 20),
        name="pack",
    )(ids, table)


def attend_kernel(heads, first_group, live_ref, rows_ref, w_ref, q_ref, g_ref, *rest):
    att_ref, qg_ref, term_ref, kv, kv_grad, q_turned, g_turned = rest[-7:]
    scale = HD**-0.5
    width = heads * HD
    step = pl.program_id(0)
    live = (live_ref[0] > 0) | (step + first_group > 0)
    grads = jnp.where(live, g_ref[...], jnp.zeros((), BF16))
    q_turned[...] = jnp.transpose(q_ref[...])
    g_turned[...] = jnp.transpose(grads)

    def project(base):
        rows = rows_ref[:, step].reshape(-1, rows_ref.shape[-1])
        for start in (base * HD, width + base * HD):
            part = slice(start, start + HEAD_BATCH * HD)
            kv[:, part] = dot(rows, w_ref[:, part], 1, 0).astype(BF16)

    project(0)
    for base in range(0, heads, HEAD_BATCH):
        keys = [slice(h * HD, (h + 1) * HD) for h in range(base, base + HEAD_BATCH)]
        values = [slice(width + h * HD, width + (h + 1) * HD) for h in range(base, base + HEAD_BATCH)]
        scores = [dot(q_ref[:, k], kv[:, k], 1, 1) * scale for k in keys]
        grad_probs = [dot(grads[:, k], kv[:, v], 1, 1) for k, v in zip(keys, values)]
        if base + HEAD_BATCH < heads:
            project(base + HEAD_BATCH)
        raised = [jnp.exp(s - jnp.max(s, axis=-1, keepdims=True)) for s in scores]
        probs = [e / jnp.sum(e, axis=-1, keepdims=True) for e in raised]
        halves = [p.astype(BF16) for p in probs]
        score_grads = [
            (p * (gp - jnp.sum(p * gp, axis=-1, keepdims=True))).astype(BF16)
            for p, gp in zip(probs, grad_probs)
        ]
        for k, v, half, sg in zip(keys, values, halves, score_grads):
            att_ref[:, k] = jnp.where(live, dot(half, kv[:, v], 1, 0), 0.0).astype(BF16)
            qg_ref[:, k] = (dot(sg, kv[:, k], 1, 0) * scale).astype(BF16)
            kv_grad[k, :] = (dot(q_turned[k, :], sg, 1, 0) * scale).astype(BF16)
            kv_grad[v, :] = dot(g_turned[k, :], half, 1, 0).astype(BF16)
    terms = jnp.transpose(dot(w_ref[...], kv_grad[...], 1, 0)).astype(BF16)
    term_ref[...] = terms.reshape(term_ref.shape)


def in_hbm(*arrays):
    return [pltpu.with_memory_space_constraint(a, pltpu.HBM) for a in arrays]


def attend(live, rows, weight, queries, grads, before, first_group, line):
    slices, chunk_groups, _, enc = rows.shape
    tokens, width = queries.shape
    keys = slices * 16
    block = pl.BlockSpec((GROUP, width), lambda i, l: (i + first_group, 0))
    flops = chunk_groups * (2 * 2 * keys * enc * 2 * width + 6 * 2 * GROUP * keys * width)
    return pl.pallas_call(
        functools.partial(attend_kernel, width // HD, first_group),
        out_shape=[
            pltpu.HBM((tokens, width), BF16),
            pltpu.HBM((tokens, width), BF16),
            pltpu.HBM((line, chunk_groups, keys // line, enc), BF16),
        ],
        grid_spec=pltpu.PrefetchScalarGridSpec(
            num_scalar_prefetch=1,
            grid=(chunk_groups,),
            in_specs=[
                pl.BlockSpec(memory_space=pltpu.VMEM),
                pl.BlockSpec(weight.shape, lambda i, l: (0, 0), pipeline_mode=pl.Buffered(1)),
                block,
                block,
            ]
            + [pl.BlockSpec(memory_space=pl.ANY)] * len(before),
            out_specs=[
                block,
                block,
                pl.BlockSpec((line, 1, keys // line, enc), lambda i, l: (0, i, 0, 0)),
            ],
            scratch_shapes=[
                pltpu.VMEM((keys, 2 * width), BF16),
                pltpu.VMEM((2 * width, keys), BF16),
                pltpu.VMEM((width, GROUP), BF16),
                pltpu.VMEM((width, GROUP), BF16),
            ],
        ),
        input_output_aliases={5 + n: n for n in range(len(before))},
        cost_estimate=pl.CostEstimate(flops=flops, bytes_accessed=16 << 20, transcendentals=0),
        compiler_params=pltpu.CompilerParams(vmem_limit_bytes=32 << 20),
        name="attend",
    )(live, rows, *in_hbm(weight, queries, grads, *before))


def exchange(block, axes):
    return lax.all_to_all(block, axes, split_axis=0, concat_axis=0, tiled=True)


def body(queries, database, kv_weight, neighbours, out_grad):
    seq_count = lax.axis_size(SEQ)
    seq_index = lax.axis_index(SEQ)
    x_count, z_count = lax.axis_size("x"), lax.axis_size("z")
    dp_count = lax.axis_size(DP)
    line = lax.axis_size(LINE)
    group_count = neighbours.shape[1]
    ref_count = 2 * group_count
    held, row_tokens, enc = database.shape
    width = queries.shape[2]
    chunk_groups = group_count // CHUNKS
    own_tokens = row_tokens // line

    slice_rows, lane_tiles = row_tokens // seq_count, enc // LANES
    slices = database.reshape(held, seq_count, slice_rows, lane_tiles, LANES)
    slices = slices.transpose(1, 0, 3, 2, 4).reshape(seq_count, held * lane_tiles, slice_rows, LANES)
    id_tile = jnp.pad(
        neighbours.reshape(1, ref_count).astype(BF16), ((0, slice_rows - 1), (0, LANES - ref_count))
    )
    id_tile = jnp.broadcast_to(id_tile, (seq_count, 1, slice_rows, LANES))
    table = exchange(jnp.concatenate([slices, id_tile], axis=1), SEQ)
    all_ids = table[:, held * lane_tiles, 0, :ref_count].astype(jnp.int32).reshape(-1)
    windows = jnp.concatenate([all_ids[:2], all_ids[:-2]])

    live = (seq_index > 0).astype(jnp.int32).reshape(1)
    packed = [
        pack(windows, table, enc, c * chunk_groups, group_count, chunk_groups) for c in range(CHUNKS)
    ]
    rows = [exchange(p, SEQ) for p in packed]

    z_index = lax.axis_index("z")
    column = lax.dynamic_index_in_dim(
        windows.reshape(x_count, z_count, ref_count), z_index, axis=1, keepdims=False
    )
    column_live = (
        (jnp.arange(x_count)[:, None] > 0) | (z_index > 0) | (jnp.arange(ref_count)[None, :] >= 2)
    )
    column = jnp.where(column_live, column, -1)
    column, _ = lax.optimization_barrier((column, packed[-1]))
    line_ids = lax.all_gather(column, DP, axis=0, tiled=False).reshape(line, group_count, 2)
    keys = jnp.where(
        line_ids[..., None] >= 0, line_ids[..., None] * own_tokens + jnp.arange(own_tokens), -1
    )

    slots = seq_count * held * own_tokens
    matches = [
        (
            jnp.arange(slots)[:, None]
            == keys[:, c * chunk_groups : (c + 1) * chunk_groups].reshape(1, -1)
        ).astype(BF16)
        for c in range(CHUNKS)
    ]
    live, matches = lax.optimization_barrier((live, matches))

    done = ()
    total = jnp.zeros((slots, enc), F32)
    for c in range(CHUNKS):
        *done, terms = attend(
            live, rows[c], kv_weight, queries[0], out_grad[0], done, c * chunk_groups, line
        )
        back = exchange(terms, LINE)
        total = total + jnp.dot(matches[c], back.reshape(-1, enc), preferred_element_type=F32)
    owned = exchange(total.astype(BF16).reshape(seq_count, held * own_tokens, enc), SEQ)
    owned = owned.reshape(x_count, z_count, held, own_tokens, enc).astype(F32).sum(axis=1)
    row_grad = owned.transpose(1, 0, 2, 3).reshape(held, x_count * own_tokens, enc)
    return done[0][None], done[1][None], row_grad


def solution(mesh):
    split = Mesh(mesh.devices.reshape(4, 2, 4, 4), ("y", "c", "x", "z"))
    return jax.shard_map(
        body,
        mesh=split,
        in_specs=(
            P(DP, SEQ, None),
            P(SEQ, None, None),
            P(),
            P(DP, SEQ, None),
            P(DP, SEQ, None),
        ),
        out_specs=(P(DP, SEQ, None), P(DP, SEQ, None), P(SEQ, DP, None)),
        check_vma=False,
    )
```

```python
import functools

import jax
import jax.numpy as jnp
from jax import lax
from jax.experimental import pallas as pl
from jax.experimental.pallas import tpu as pltpu
from jax.sharding import Mesh
from jax.sharding import PartitionSpec as P

HD = 128
GROUP = 64
SEQ = ("x", "z")
DP = ("y", "c")
LINE = ("y", "c", "x")
CHUNKS = 2
HEAD_BATCH = 4
LANES = 128
F32 = jnp.float32
BF16 = jnp.bfloat16


def dot(a, b, ca, cb):
    return lax.dot_general(a, b, (((ca,), (cb,)), ((), ())), preferred_element_type=F32)


def spread_kernel(core_ref, ids_ref, rows_ref, out_ref):
    half, tokens, enc = rows_ref.shape
    lane_tiles = enc // LANES
    lanes = lax.broadcasted_iota(jnp.int32, (8, LANES), 1)
    ids = jnp.zeros((8, LANES), jnp.int32)
    for r in range(ids_ref.shape[0]):
        ids = jnp.where(lanes == r, ids_ref[r], ids)
    ids = ids.astype(F32).astype(BF16)
    for pair in range(tokens // 16):
        for j in range(half):
            for t in range(lane_tiles):
                rows = rows_ref[j, 16 * pair : 16 * pair + 16, t * LANES : (t + 1) * LANES].astype(F32)
                out_ref[2 * pair, j * lane_tiles + t] = rows[:8].astype(BF16)
                out_ref[2 * pair + 1, j * lane_tiles + t] = rows[8:].astype(BF16)
        out_ref[2 * pair, half * lane_tiles] = ids
        out_ref[2 * pair + 1, half * lane_tiles] = ids


def spread(core, ids, database, dests):
    held, tokens, enc = database.shape
    half = held // 2
    out = (dests, half * (enc // LANES) + 1, tokens // dests, LANES)
    return pl.pallas_call(
        spread_kernel,
        out_shape=pltpu.HBM(out, BF16),
        grid_spec=pltpu.PrefetchScalarGridSpec(
            num_scalar_prefetch=2,
            grid=(1,),
            in_specs=[pl.BlockSpec((half, tokens, enc), lambda i, core, ids: (core[0], 0, 0))],
            out_specs=pl.BlockSpec(out, lambda i, core, ids: (0, 0, 0, 0)),
        ),
        compiler_params=pltpu.CompilerParams(vmem_limit_bytes=16 << 20),
        name="spread",
    )(core, ids, *in_hbm(database))


def pack_kernel(
    first_group, group_count, chunk_groups, lane_tiles, core_ref, ids_ref, own_ref, other_ref, out_ref
):
    def load(ref_id, t):
        at = (ref_id >> 2, (ref_id & 1) * lane_tiles + t)
        own = ((ref_id >> 1) & 1) == core_ref[0]
        return jnp.where(own, own_ref[at].astype(F32), other_ref[at].astype(F32))

    def per_dest(dest, carry):
        for g in range(chunk_groups):
            at = dest * 2 * group_count + 2 * (first_group + g)
            first, second = ids_ref[at], ids_ref[at + 1]
            for t in range(lane_tiles):
                a, b = load(first, t), load(second, t)
                out_ref[dest, g, :, t * LANES : (t + 1) * LANES] = jnp.concatenate(
                    [a[:4], b[:4], a[4:], b[4:]], axis=0
                ).astype(BF16)
        return carry

    lax.fori_loop(0, out_ref.shape[0], per_dest, 0)


def pack(core, ids, own, other, enc, first_group, group_count, chunk_groups):
    dests = own.shape[0]
    return pl.pallas_call(
        functools.partial(pack_kernel, first_group, group_count, chunk_groups, enc // LANES),
        out_shape=jax.ShapeDtypeStruct((dests, chunk_groups, 16, enc), BF16),
        in_specs=[
            pl.BlockSpec(memory_space=pltpu.SMEM),
            pl.BlockSpec(memory_space=pltpu.SMEM),
            pl.BlockSpec(memory_space=pltpu.VMEM),
            pl.BlockSpec(memory_space=pltpu.VMEM),
        ],
        out_specs=pl.BlockSpec(memory_space=pltpu.VMEM),
        compiler_params=pltpu.CompilerParams(vmem_limit_bytes=16 << 20),
        name="pack",
    )(core, ids, own, other)


def attend_kernel(heads, first_group, live_ref, rows_ref, w_ref, q_ref, g_ref, *rest):
    att_ref, qg_ref, term_ref, kv, kv_grad, q_turned, g_turned = rest[-7:]
    scale = HD**-0.5
    width = heads * HD
    step = pl.program_id(0)
    live = (live_ref[0] > 0) | (step + first_group > 0)
    grads = jnp.where(live, g_ref[...], jnp.zeros((), BF16))
    q_turned[...] = jnp.transpose(q_ref[...])
    g_turned[...] = jnp.transpose(grads)

    def project(base):
        rows = rows_ref[:, step].reshape(-1, rows_ref.shape[-1])
        for start in (base * HD, width + base * HD):
            part = slice(start, start + HEAD_BATCH * HD)
            kv[:, part] = dot(rows, w_ref[:, part], 1, 0).astype(BF16)

    project(0)
    for base in range(0, heads, HEAD_BATCH):
        keys = [slice(h * HD, (h + 1) * HD) for h in range(base, base + HEAD_BATCH)]
        values = [slice(width + h * HD, width + (h + 1) * HD) for h in range(base, base + HEAD_BATCH)]
        scores = [dot(q_ref[:, k], kv[:, k], 1, 1) * scale for k in keys]
        grad_probs = [dot(grads[:, k], kv[:, v], 1, 1) for k, v in zip(keys, values)]
        if base + HEAD_BATCH < heads:
            project(base + HEAD_BATCH)
        raised = [jnp.exp(s - jnp.max(s, axis=-1, keepdims=True)) for s in scores]
        probs = [e / jnp.sum(e, axis=-1, keepdims=True) for e in raised]
        halves = [p.astype(BF16) for p in probs]
        score_grads = [
            (p * (gp - jnp.sum(p * gp, axis=-1, keepdims=True))).astype(BF16)
            for p, gp in zip(probs, grad_probs)
        ]
        for k, v, half, sg in zip(keys, values, halves, score_grads):
            att_ref[:, k] = jnp.where(live, dot(half, kv[:, v], 1, 0), 0.0).astype(BF16)
            qg_ref[:, k] = (dot(sg, kv[:, k], 1, 0) * scale).astype(BF16)
            kv_grad[k, :] = (dot(q_turned[k, :], sg, 1, 0) * scale).astype(BF16)
            kv_grad[v, :] = dot(g_turned[k, :], half, 1, 0).astype(BF16)
    terms = jnp.transpose(dot(w_ref[...], kv_grad[...], 1, 0)).astype(BF16)
    term_ref[...] = terms.reshape(term_ref.shape)


def in_hbm(*arrays):
    return [pltpu.with_memory_space_constraint(a, pltpu.HBM) for a in arrays]


def attend(live, rows, weight, queries, grads, before, first_group, line):
    slices, chunk_groups, _, enc = rows.shape
    tokens, width = queries.shape
    keys = slices * 16
    block = pl.BlockSpec((GROUP, width), lambda i, l: (i + first_group, 0))
    flops = chunk_groups * (2 * 2 * keys * enc * 2 * width + 6 * 2 * GROUP * keys * width)
    return pl.pallas_call(
        functools.partial(attend_kernel, width // HD, first_group),
        out_shape=[
            pltpu.HBM((tokens, width), BF16),
            pltpu.HBM((tokens, width), BF16),
            pltpu.HBM((line, chunk_groups, keys // line, enc), BF16),
        ],
        grid_spec=pltpu.PrefetchScalarGridSpec(
            num_scalar_prefetch=1,
            grid=(chunk_groups,),
            in_specs=[
                pl.BlockSpec(memory_space=pltpu.VMEM),
                pl.BlockSpec(weight.shape, lambda i, l: (0, 0), pipeline_mode=pl.Buffered(1)),
                block,
                block,
            ]
            + [pl.BlockSpec(memory_space=pl.ANY)] * len(before),
            out_specs=[
                block,
                block,
                pl.BlockSpec((line, 1, keys // line, enc), lambda i, l: (0, i, 0, 0)),
            ],
            scratch_shapes=[
                pltpu.VMEM((keys, 2 * width), BF16),
                pltpu.VMEM((2 * width, keys), BF16),
                pltpu.VMEM((width, GROUP), BF16),
                pltpu.VMEM((width, GROUP), BF16),
            ],
        ),
        input_output_aliases={5 + n: n for n in range(len(before))},
        cost_estimate=pl.CostEstimate(flops=flops, bytes_accessed=16 << 20, transcendentals=0),
        compiler_params=pltpu.CompilerParams(vmem_limit_bytes=32 << 20),
        name="attend",
    )(live, rows, *in_hbm(weight, queries, grads, *before))


def exchange(block, axes):
    return lax.all_to_all(block, axes, split_axis=0, concat_axis=0, tiled=True)


def body(queries, database, kv_weight, neighbours, out_grad):
    seq_count = lax.axis_size(SEQ)
    seq_index = lax.axis_index(SEQ)
    x_count, z_count = lax.axis_size("x"), lax.axis_size("z")
    dp_count = lax.axis_size(DP)
    line = lax.axis_size(LINE)
    group_count = neighbours.shape[1]
    ref_count = 2 * group_count
    held, row_tokens, enc = database.shape
    width = queries.shape[2]
    chunk_groups = group_count // CHUNKS
    own_tokens = row_tokens // line

    core = lax.axis_index("c").astype(jnp.int32).reshape(1)
    own = exchange(spread(core, neighbours.reshape(ref_count), database, seq_count), SEQ)
    other = lax.ppermute(own, "c", [(0, 1), (1, 0)])
    id_tile = held // 2 * (enc // LANES)
    all_ids = own[:, id_tile, 0, :ref_count].astype(jnp.int32).reshape(-1)
    windows = jnp.concatenate([all_ids[:2], all_ids[:-2]])

    live = (seq_index > 0).astype(jnp.int32).reshape(1)
    packed = [
        pack(core, windows, own, other, enc, c * chunk_groups, group_count, chunk_groups)
        for c in range(CHUNKS)
    ]
    rows = [exchange(p, SEQ) for p in packed]

    z_index = lax.axis_index("z")
    column = lax.dynamic_index_in_dim(
        windows.reshape(x_count, z_count, ref_count), z_index, axis=1, keepdims=False
    )
    column_live = (
        (jnp.arange(x_count)[:, None] > 0) | (z_index > 0) | (jnp.arange(ref_count)[None, :] >= 2)
    )
    column = jnp.where(column_live, column, -1)
    column, _ = lax.optimization_barrier((column, packed[-1]))
    line_ids = lax.all_gather(column, DP, axis=0, tiled=False).reshape(line, group_count, 2)
    keys = jnp.where(
        line_ids[..., None] >= 0, line_ids[..., None] * own_tokens + jnp.arange(own_tokens), -1
    )

    slots = seq_count * held * own_tokens
    matches = [
        (
            jnp.arange(slots)[:, None]
            == keys[:, c * chunk_groups : (c + 1) * chunk_groups].reshape(1, -1)
        ).astype(BF16)
        for c in range(CHUNKS)
    ]
    live, matches = lax.optimization_barrier((live, matches))

    done = ()
    total = jnp.zeros((slots, enc), F32)
    for c in range(CHUNKS):
        *done, terms = attend(
            live, rows[c], kv_weight, queries[0], out_grad[0], done, c * chunk_groups, line
        )
        back = exchange(terms, LINE)
        total = total + jnp.dot(matches[c], back.reshape(-1, enc), preferred_element_type=F32)
    owned = exchange(total.astype(BF16).reshape(seq_count, held * own_tokens, enc), SEQ)
    owned = owned.reshape(x_count, z_count, held, own_tokens, enc).astype(F32).sum(axis=1)
    row_grad = owned.transpose(1, 0, 2, 3).reshape(held, x_count * own_tokens, enc)
    return done[0][None], done[1][None], row_grad


def solution(mesh):
    split = Mesh(mesh.devices.reshape(4, 2, 4, 4), ("y", "c", "x", "z"))
    return jax.shard_map(
        body,
        mesh=split,
        in_specs=(
            P(DP, SEQ, None),
            P(SEQ, None, None),
            P(),
            P(DP, SEQ, None),
            P(DP, SEQ, None),
        ),
        out_specs=(P(DP, SEQ, None), P(DP, SEQ, None), P(SEQ, DP, None)),
        check_vma=False,
    )
```

```python
import functools

import jax
import jax.numpy as jnp
from jax import lax
from jax.experimental import pallas as pl
from jax.experimental.pallas import tpu as pltpu
from jax.sharding import Mesh
from jax.sharding import PartitionSpec as P

HD = 128
GROUP = 64
SEQ = ("x", "z")
DP = ("y", "c")
LINE = ("y", "c", "x")
CHUNKS = 2
HEAD_BATCH = 8
LANES = 128
F32 = jnp.float32
BF16 = jnp.bfloat16


def dot(a, b, ca, cb):
    return lax.dot_general(a, b, (((ca,), (cb,)), ((), ())), preferred_element_type=F32)


def spread_kernel(core_ref, ids_ref, rows_ref, out_ref):
    half, tokens, enc = rows_ref.shape
    lane_tiles = enc // LANES
    lanes = lax.broadcasted_iota(jnp.int32, (8, LANES), 1)
    ids = jnp.zeros((8, LANES), jnp.int32)
    for g in range(ids_ref.shape[1]):
        for r in range(2):
            ids = jnp.where(lanes == 2 * g + r, ids_ref[r, g], ids)
    ids = ids.astype(F32).astype(BF16)
    for pair in range(tokens // 16):
        for j in range(half):
            for t in range(lane_tiles):
                rows = rows_ref[j, 16 * pair : 16 * pair + 16, t * LANES : (t + 1) * LANES].astype(F32)
                out_ref[2 * pair, j * lane_tiles + t] = rows[:8].astype(BF16)
                out_ref[2 * pair + 1, j * lane_tiles + t] = rows[8:].astype(BF16)
        out_ref[2 * pair, half * lane_tiles] = ids
        out_ref[2 * pair + 1, half * lane_tiles] = ids


def spread(core, ids, database, dests):
    held, tokens, enc = database.shape
    half = held // 2
    out = (dests, half * (enc // LANES) + 1, tokens // dests, LANES)
    return pl.pallas_call(
        spread_kernel,
        out_shape=pltpu.HBM(out, BF16),
        grid_spec=pltpu.PrefetchScalarGridSpec(
            num_scalar_prefetch=2,
            grid=(1,),
            in_specs=[pl.BlockSpec((half, tokens, enc), lambda i, core, ids: (core[0], 0, 0))],
            out_specs=pl.BlockSpec(out, lambda i, core, ids: (0, 0, 0, 0)),
        ),
        compiler_params=pltpu.CompilerParams(vmem_limit_bytes=16 << 20),
        name="spread",
    )(core, ids, *in_hbm(database))


def pack_kernel(
    first_group, group_count, chunk_groups, lane_tiles, core_ref, ids_ref, own_ref, other_ref, out_ref
):
    def load(ref_id, t):
        at = (ref_id >> 2, (ref_id & 1) * lane_tiles + t)
        own = ((ref_id >> 1) & 1) == core_ref[0]
        return jnp.where(own, own_ref[at].astype(F32), other_ref[at].astype(F32))

    def per_dest(dest, carry):
        for g in range(chunk_groups):
            at = dest * 2 * group_count + 2 * (first_group + g)
            first, second = ids_ref[at], ids_ref[at + 1]
            for t in range(lane_tiles):
                a, b = load(first, t), load(second, t)
                out_ref[dest, g, :, t * LANES : (t + 1) * LANES] = jnp.concatenate(
                    [a[:4], b[:4], a[4:], b[4:]], axis=0
                ).astype(BF16)
        return carry

    lax.fori_loop(0, out_ref.shape[0], per_dest, 0)


def pack(core, ids, own, other, enc, first_group, group_count, chunk_groups):
    dests = own.shape[0]
    return pl.pallas_call(
        functools.partial(pack_kernel, first_group, group_count, chunk_groups, enc // LANES),
        out_shape=jax.ShapeDtypeStruct((dests, chunk_groups, 16, enc), BF16),
        in_specs=[
            pl.BlockSpec(memory_space=pltpu.SMEM),
            pl.BlockSpec(memory_space=pltpu.SMEM),
            pl.BlockSpec(memory_space=pltpu.VMEM),
            pl.BlockSpec(memory_space=pltpu.VMEM),
        ],
        out_specs=pl.BlockSpec(memory_space=pltpu.VMEM),
        compiler_params=pltpu.CompilerParams(vmem_limit_bytes=16 << 20),
        name="pack",
    )(core, ids, own, other)


def attend_kernel(heads, first_group, groups, live_ref, rows_ref, w_hbm, q_hbm, g_hbm, *rest):
    att_hbm, qg_hbm, term_hbm = rest[-17:-14]
    w, q, g, att, qg, term, kv, kv_grad, total, q_turned, g_turned = rest[-14:-3]
    w_sems, in_sems, out_sems = rest[-3:]
    scale = HD**-0.5
    width = heads * HD
    span = HEAD_BATCH * HD
    batches = heads // HEAD_BATCH

    def copy(source, target, sem):
        started = pltpu.make_async_copy(source, target, sem)
        started.start()
        return started

    def outer(ref, j):
        return ref.at[pl.ds((first_group + j) * GROUP, GROUP)]

    def inner(ref, j):
        return ref.at[pl.ds(j * GROUP, GROUP)]

    def halves_of(b):
        return slice(b * span, (b + 1) * span), slice(width + b * span, width + (b + 1) * span)

    def load(j):
        return [
            copy(outer(q_hbm, j), inner(q, j), in_sems.at[j, 0]),
            copy(outer(g_hbm, j), inner(g, j), in_sems.at[j, 1]),
        ]

    loads, weights, stores = [], [], []
    for b in range(batches):
        weights.append([copy(w_hbm.at[:, p], w.at[:, p], w_sems.at[b, i]) for i, p in enumerate(halves_of(b))])
        if b == 0:
            loads.append(load(0))
    loads += [load(j) for j in range(1, groups)]

    def project(j, b):
        if j == 0:
            for started in weights[b]:
                started.wait()
        rows = rows_ref[:, j].reshape(-1, rows_ref.shape[-1])
        for part in halves_of(b):
            kv[j % 2, :, part] = dot(rows, w[:, part], 1, 0).astype(BF16)

    def back_project(j, b):
        k, v = halves_of(b)
        summed = dot(w[:, k], kv_grad[j % 2, k, :], 1, 0) + dot(w[:, v], kv_grad[j % 2, v, :], 1, 0)
        if b > 0:
            summed = total[...] + summed
        if b + 1 < batches:
            total[...] = summed
        else:
            term[:, j] = jnp.transpose(summed).astype(BF16).reshape(term.shape[0], *term.shape[2:])
            stores.append(copy(term.at[:, j], term_hbm.at[:, j], out_sems.at[j, 2]))

    items = [(j, b) for j in range(groups) for b in range(batches)]
    project(*items[0])
    for n, (j, b) in enumerate(items):
        here = slice(j * GROUP, (j + 1) * GROUP)
        live = live_ref[0] > 0 if first_group + j == 0 else None
        if b == 0:
            for started in loads[j]:
                started.wait()
            if live is not None:
                g[here] = jnp.where(live, g[here], jnp.zeros((), BF16))
            q_turned[j % 2] = jnp.transpose(q[here])
            g_turned[j % 2] = jnp.transpose(g[here])
        of_batch = range(b * HEAD_BATCH, (b + 1) * HEAD_BATCH)
        keys = [slice(h * HD, (h + 1) * HD) for h in of_batch]
        values = [slice(width + h * HD, width + (h + 1) * HD) for h in of_batch]
        held, held_grad = kv.at[j % 2], kv_grad.at[j % 2]
        scores = [dot(q[here, k], held[:, k], 1, 1) * scale for k in keys]
        grad_probs = [dot(g[here, k], held[:, v], 1, 1) for k, v in zip(keys, values)]
        if n + 1 < len(items):
            project(*items[n + 1])
        if n > 0:
            back_project(*items[n - 1])
        raised = [jnp.exp(s - jnp.max(s, axis=-1, keepdims=True)) for s in scores]
        probs = [e / jnp.sum(e, axis=-1, keepdims=True) for e in raised]
        halves = [p.astype(BF16) for p in probs]
        score_grads = [
            (p * (gp - jnp.sum(p * gp, axis=-1, keepdims=True))).astype(BF16)
            for p, gp in zip(probs, grad_probs)
        ]
        for k, v, half, sg in zip(keys, values, halves, score_grads):
            attended = dot(half, held[:, v], 1, 0)
            if live is not None:
                attended = jnp.where(live, attended, 0.0)
            att[here, k] = attended.astype(BF16)
            qg[here, k] = (dot(sg, held[:, k], 1, 0) * scale).astype(BF16)
            held_grad[k, :] = (dot(q_turned[j % 2, k, :], sg, 1, 0) * scale).astype(BF16)
            held_grad[v, :] = dot(g_turned[j % 2, k, :], half, 1, 0).astype(BF16)
        if b + 1 == batches:
            stores.append(copy(inner(att, j), outer(att_hbm, j), out_sems.at[j, 0]))
            stores.append(copy(inner(qg, j), outer(qg_hbm, j), out_sems.at[j, 1]))
    back_project(*items[-1])
    for started in stores:
        started.wait()


def in_hbm(*arrays):
    return [pltpu.with_memory_space_constraint(a, pltpu.HBM) for a in arrays]


def attend(live, rows, weight, queries, grads, before, first_group, line):
    slices, groups, _, enc = rows.shape
    tokens, width = queries.shape
    keys = slices * 16
    terms = (line, groups, keys // line, enc)
    batches = width // HD // HEAD_BATCH
    hbm = pl.BlockSpec(memory_space=pltpu.HBM)
    own = pltpu.VMEM((groups * GROUP, width), BF16)
    flops = groups * (2 * 2 * keys * enc * 2 * width + 6 * 2 * GROUP * keys * width)
    return pl.pallas_call(
        functools.partial(attend_kernel, width // HD, first_group, groups),
        out_shape=[
            pltpu.HBM((tokens, width), BF16),
            pltpu.HBM((tokens, width), BF16),
            pltpu.HBM(terms, BF16),
        ],
        in_specs=[pl.BlockSpec(memory_space=pltpu.SMEM), pl.BlockSpec(memory_space=pltpu.VMEM)]
        + [hbm] * (3 + len(before)),
        out_specs=[hbm] * 3,
        scratch_shapes=[
            pltpu.VMEM(weight.shape, BF16),
            own,
            own,
            own,
            own,
            pltpu.VMEM(terms, BF16),
            pltpu.VMEM((2, keys, 2 * width), BF16),
            pltpu.VMEM((2, 2 * width, keys), BF16),
            pltpu.VMEM((enc, keys), F32),
            pltpu.VMEM((2, width, GROUP), BF16),
            pltpu.VMEM((2, width, GROUP), BF16),
            pltpu.SemaphoreType.DMA((batches, 2)),
            pltpu.SemaphoreType.DMA((groups, 2)),
            pltpu.SemaphoreType.DMA((groups, 3)),
        ],
        input_output_aliases={5 + n: n for n in range(len(before))},
        cost_estimate=pl.CostEstimate(flops=flops, bytes_accessed=16 << 20, transcendentals=0),
        compiler_params=pltpu.CompilerParams(vmem_limit_bytes=40 << 20),
        name="attend",
    )(live, rows, *in_hbm(weight, queries, grads, *before))


def exchange(block, axes):
    return lax.all_to_all(block, axes, split_axis=0, concat_axis=0, tiled=True)


def body(queries, database, kv_weight, neighbours, out_grad):
    seq_count = lax.axis_size(SEQ)
    seq_index = lax.axis_index(SEQ)
    x_count, z_count = lax.axis_size("x"), lax.axis_size("z")
    dp_count = lax.axis_size(DP)
    line = lax.axis_size(LINE)
    group_count = neighbours.shape[1]
    ref_count = 2 * group_count
    held, row_tokens, enc = database.shape
    width = queries.shape[2]
    chunk_groups = group_count // CHUNKS
    own_tokens = row_tokens // line

    core = lax.axis_index("c").astype(jnp.int32).reshape(1)
    own = exchange(spread(core, neighbours[0].T, database, seq_count), SEQ)
    other = lax.ppermute(own, "c", [(0, 1), (1, 0)])
    id_tile = held // 2 * (enc // LANES)
    all_ids = own[:, id_tile, 0, :ref_count].astype(jnp.int32).reshape(-1)
    windows = jnp.concatenate([all_ids[:2], all_ids[:-2]])

    live = (seq_index > 0).astype(jnp.int32).reshape(1)
    packed = [
        pack(core, windows, own, other, enc, c * chunk_groups, group_count, chunk_groups)
        for c in range(CHUNKS)
    ]
    rows = [exchange(p, SEQ) for p in packed]

    z_index = lax.axis_index("z")
    column = lax.dynamic_index_in_dim(
        windows.reshape(x_count, z_count, ref_count), z_index, axis=1, keepdims=False
    )
    column_live = (
        (jnp.arange(x_count)[:, None] > 0) | (z_index > 0) | (jnp.arange(ref_count)[None, :] >= 2)
    )
    column = jnp.where(column_live, column, -1)
    column, _ = lax.optimization_barrier((column, packed[-1]))
    line_ids = lax.all_gather(column, DP, axis=0, tiled=False).reshape(line, group_count, 2)
    keys = jnp.where(
        line_ids[..., None] >= 0, line_ids[..., None] * own_tokens + jnp.arange(own_tokens), -1
    )

    slots = seq_count * held * own_tokens
    matches = [
        (
            jnp.arange(slots)[:, None]
            == keys[:, c * chunk_groups : (c + 1) * chunk_groups].reshape(1, -1)
        ).astype(BF16)
        for c in range(CHUNKS)
    ]
    live, matches = lax.optimization_barrier((live, matches))

    done = ()
    total = jnp.zeros((slots, enc), F32)
    for c in range(CHUNKS):
        *done, terms = attend(
            live, rows[c], kv_weight, queries[0], out_grad[0], done, c * chunk_groups, line
        )
        back = exchange(terms, LINE)
        total = total + jnp.dot(matches[c], back.reshape(-1, enc), preferred_element_type=F32)
    owned = exchange(total.astype(BF16).reshape(seq_count, held * own_tokens, enc), SEQ)
    owned = owned.reshape(x_count, z_count, held, own_tokens, enc).astype(F32).sum(axis=1)
    row_grad = owned.transpose(1, 0, 2, 3).reshape(held, x_count * own_tokens, enc)
    return done[0][None], done[1][None], row_grad


def solution(mesh):
    split = Mesh(mesh.devices.reshape(4, 2, 4, 4), ("y", "c", "x", "z"))
    return jax.shard_map(
        body,
        mesh=split,
        in_specs=(
            P(DP, SEQ, None),
            P(SEQ, None, None),
            P(),
            P(DP, SEQ, None),
            P(DP, SEQ, None),
        ),
        out_specs=(P(DP, SEQ, None), P(DP, SEQ, None), P(SEQ, DP, None)),
        check_vma=False,
    )
```

```python
import functools

import jax
import jax.numpy as jnp
from jax import lax
from jax.experimental import pallas as pl
from jax.experimental.pallas import tpu as pltpu
from jax.sharding import Mesh
from jax.sharding import PartitionSpec as P

HD = 128
GROUP = 64
SEQ = ("x", "z")
DP = ("y", "c")
LINE = ("y", "x")
CHUNKS = 2
HEAD_BATCH = 8
LANES = 128
F32 = jnp.float32
BF16 = jnp.bfloat16


def dot(a, b, ca, cb):
    return lax.dot_general(a, b, (((ca,), (cb,)), ((), ())), preferred_element_type=F32)


def spread_kernel(core_ref, ids_ref, rows_ref, out_ref):
    half, tokens, enc = rows_ref.shape
    lane_tiles = enc // LANES
    lanes = lax.broadcasted_iota(jnp.int32, (8, LANES), 1)
    ids = jnp.zeros((8, LANES), jnp.int32)
    for g in range(ids_ref.shape[1]):
        for r in range(2):
            ids = jnp.where(lanes == 2 * g + r, ids_ref[r, g], ids)
    ids = ids.astype(F32).astype(BF16)
    for y in range(tokens // 32):
        for j in range(half):
            for t in range(lane_tiles):
                lane = slice(t * LANES, (t + 1) * LANES)
                a = rows_ref[j, 32 * y : 32 * y + 16, lane].astype(F32)
                b = rows_ref[j, 32 * y + 16 : 32 * y + 32, lane].astype(F32)
                for x in range(4):
                    piece = jnp.concatenate([a[4 * x : 4 * x + 4], b[4 * x : 4 * x + 4]], axis=0)
                    out_ref[4 * y + x, j * lane_tiles + t] = piece.astype(BF16)
    for dest in range(out_ref.shape[0]):
        out_ref[dest, half * lane_tiles] = ids


def spread(core, ids, database, dests):
    held, tokens, enc = database.shape
    half = held // 2
    out = (dests, half * (enc // LANES) + 1, tokens // dests, LANES)
    return pl.pallas_call(
        spread_kernel,
        out_shape=pltpu.HBM(out, BF16),
        grid_spec=pltpu.PrefetchScalarGridSpec(
            num_scalar_prefetch=2,
            grid=(1,),
            in_specs=[pl.BlockSpec((half, tokens, enc), lambda i, core, ids: (core[0], 0, 0))],
            out_specs=pl.BlockSpec(out, lambda i, core, ids: (0, 0, 0, 0)),
        ),
        compiler_params=pltpu.CompilerParams(vmem_limit_bytes=16 << 20),
        name="spread",
    )(core, *in_hbm(ids, database))


def pack_kernel(
    first_group, group_count, chunk_groups, lane_tiles, core_ref, ids_ref, own_ref, other_ref, out_ref
):
    def load(ref_id, t):
        at = (ref_id >> 2, (ref_id & 1) * lane_tiles + t)
        own = ((ref_id >> 1) & 1) == core_ref[0]
        return jnp.where(own, own_ref[at].astype(F32), other_ref[at].astype(F32))

    def per_dest(dest, carry):
        for g in range(chunk_groups):
            at = dest * 2 * group_count + 2 * (first_group + g)
            first, second = ids_ref[at], ids_ref[at + 1]
            for t in range(lane_tiles):
                a, b = load(first, t), load(second, t)
                out_ref[dest, g, :, t * LANES : (t + 1) * LANES] = jnp.concatenate(
                    [a[:4], b[:4], a[4:], b[4:]], axis=0
                ).astype(BF16)
        return carry

    lax.fori_loop(0, out_ref.shape[0], per_dest, 0)


def pack(core, ids, own, other, enc, first_group, group_count, chunk_groups):
    dests = own.shape[0]
    return pl.pallas_call(
        functools.partial(pack_kernel, first_group, group_count, chunk_groups, enc // LANES),
        out_shape=jax.ShapeDtypeStruct((dests, chunk_groups, 16, enc), BF16),
        in_specs=[
            pl.BlockSpec(memory_space=pltpu.SMEM),
            pl.BlockSpec(memory_space=pltpu.SMEM),
            pl.BlockSpec(memory_space=pltpu.VMEM),
            pl.BlockSpec(memory_space=pltpu.VMEM),
        ],
        out_specs=pl.BlockSpec(memory_space=pltpu.VMEM),
        compiler_params=pltpu.CompilerParams(vmem_limit_bytes=16 << 20),
        name="pack",
    )(core, ids, own, other)


def attend_kernel(heads, first_group, live_ref, rows_ref, w_ref, q_ref, g_ref, *rest):
    att_ref, qg_ref, term_ref, kv, kv_grad, q_pair, g_pair, q_turned, g_turned = rest[-9:]
    scale = HD**-0.5
    width = heads * HD
    span = HEAD_BATCH * HD
    step = pl.program_id(0)
    live = (live_ref[0] > 0) | (step + first_group > 0)

    @pl.when(step == 0)
    def _():
        for ref in (q_pair, g_pair, q_turned, g_turned):
            ref[...] = jnp.zeros(ref.shape, BF16)

    queries = q_ref[...]
    grads = jnp.where(live, g_ref[...], jnp.zeros((), BF16))
    turned = jnp.transpose(queries), jnp.transpose(grads)
    for h in range(heads):
        c = slice(h * HD, (h + 1) * HD)
        r = slice(h * GROUP, (h + 1) * GROUP)
        in_pair = slice(h % 2 * HD, (h % 2 + 1) * HD)
        in_four = slice(h % 4 * GROUP, (h % 4 + 1) * GROUP)
        q_pair[r, in_pair] = queries[:, c]
        g_pair[r, in_pair] = grads[:, c]
        q_turned[c, in_four] = turned[0][c]
        g_turned[c, in_four] = turned[1][c]

    def project(base):
        rows = rows_ref[:, step].reshape(-1, rows_ref.shape[-1])
        for start in (base * HD, width + base * HD):
            part = slice(start, start + span)
            kv[:, part] = dot(rows, w_ref[:, part], 1, 0).astype(BF16)

    project(0)
    for base in range(0, heads, HEAD_BATCH):
        pairs = range(base // 2, (base + HEAD_BATCH) // 2)
        keys = [slice(p * 2 * HD, (p + 1) * 2 * HD) for p in pairs]
        values = [slice(width + p * 2 * HD, width + (p + 1) * 2 * HD) for p in pairs]
        rows_of = [slice(p * 2 * GROUP, (p + 1) * 2 * GROUP) for p in pairs]
        scores = [dot(q_pair[r], kv[:, k], 1, 1) * scale for r, k in zip(rows_of, keys)]
        grad_probs = [dot(g_pair[r], kv[:, v], 1, 1) for r, v in zip(rows_of, values)]
        if base + HEAD_BATCH < heads:
            project(base + HEAD_BATCH)
        raised = [jnp.exp(s - jnp.max(s, axis=-1, keepdims=True)) for s in scores]
        probs = [e / jnp.sum(e, axis=-1, keepdims=True) for e in raised]
        halves = [p.astype(BF16) for p in probs]
        score_grads = [
            (p * (gp - jnp.sum(p * gp, axis=-1, keepdims=True))).astype(BF16)
            for p, gp in zip(probs, grad_probs)
        ]
        for p, k, v, half, sg in zip(pairs, keys, values, halves, score_grads):
            attended = dot(half, kv[:, v], 1, 0)
            query_grad = dot(sg, kv[:, k], 1, 0)
            for i in range(2):
                c = slice((2 * p + i) * HD, (2 * p + i + 1) * HD)
                at = slice(i * GROUP, (i + 1) * GROUP), slice(i * HD, (i + 1) * HD)
                att_ref[:, c] = jnp.where(live, attended[at], 0.0).astype(BF16)
                qg_ref[:, c] = (query_grad[at] * scale).astype(BF16)
        for i in range(0, len(pairs), 2):
            k = slice(keys[i].start, keys[i + 1].stop)
            v = slice(values[i].start, values[i + 1].stop)
            sg = jnp.concatenate(score_grads[i : i + 2], axis=0)
            half = jnp.concatenate(halves[i : i + 2], axis=0)
            kv_grad[k, :] = (dot(q_turned[k, :], sg, 1, 0) * scale).astype(BF16)
            kv_grad[v, :] = dot(g_turned[k, :], half, 1, 0).astype(BF16)
    terms = jnp.transpose(dot(w_ref[...], kv_grad[...], 1, 0)).astype(BF16)
    term_ref[...] = terms.reshape(term_ref.shape)


def in_hbm(*arrays):
    return [pltpu.with_memory_space_constraint(a, pltpu.HBM) for a in arrays]


def attend(live, rows, weight, queries, grads, before, first_group, line):
    slices, chunk_groups, _, enc = rows.shape
    tokens, width = queries.shape
    keys = slices * 16
    block = pl.BlockSpec((GROUP, width), lambda i, l: (i + first_group, 0))
    flops = chunk_groups * (2 * 2 * keys * enc * 2 * width + 6 * 2 * GROUP * keys * width)
    return pl.pallas_call(
        functools.partial(attend_kernel, width // HD, first_group),
        out_shape=[
            pltpu.HBM((tokens, width), BF16),
            pltpu.HBM((tokens, width), BF16),
            pltpu.HBM((line, chunk_groups, keys // line, enc), BF16),
        ],
        grid_spec=pltpu.PrefetchScalarGridSpec(
            num_scalar_prefetch=1,
            grid=(chunk_groups,),
            in_specs=[
                pl.BlockSpec(memory_space=pltpu.VMEM),
                pl.BlockSpec(weight.shape, lambda i, l: (0, 0), pipeline_mode=pl.Buffered(1)),
                block,
                block,
            ]
            + [pl.BlockSpec(memory_space=pl.ANY)] * len(before),
            out_specs=[
                block,
                block,
                pl.BlockSpec((line, 1, keys // line, enc), lambda i, l: (0, i, 0, 0)),
            ],
            scratch_shapes=[
                pltpu.VMEM((keys, 2 * width), BF16),
                pltpu.VMEM((2 * width, keys), BF16),
                pltpu.VMEM((width // 2, 2 * HD), BF16),
                pltpu.VMEM((width // 2, 2 * HD), BF16),
                pltpu.VMEM((width, 4 * GROUP), BF16),
                pltpu.VMEM((width, 4 * GROUP), BF16),
            ],
        ),
        input_output_aliases={5 + n: n for n in range(len(before))},
        cost_estimate=pl.CostEstimate(flops=flops, bytes_accessed=16 << 20, transcendentals=0),
        compiler_params=pltpu.CompilerParams(vmem_limit_bytes=32 << 20),
        name="attend",
    )(live, rows, *in_hbm(weight, queries, grads, *before))


def exchange(block, axes):
    return lax.all_to_all(block, axes, split_axis=0, concat_axis=0, tiled=True)


def body(queries, database, kv_weight, neighbours, out_grad):
    seq_count = lax.axis_size(SEQ)
    seq_index = lax.axis_index(SEQ)
    x_count, z_count = lax.axis_size("x"), lax.axis_size("z")
    dp_count = lax.axis_size(DP)
    line = lax.axis_size(LINE)
    group_count = neighbours.shape[1]
    ref_count = 2 * group_count
    held, row_tokens, enc = database.shape
    width = queries.shape[2]
    chunk_groups = group_count // CHUNKS
    own_tokens = row_tokens // (2 * line)

    core = lax.axis_index("c").astype(jnp.int32).reshape(1)
    own = exchange(spread(core, neighbours[0].T, database, seq_count), SEQ)
    other = lax.ppermute(own, "c", [(0, 1), (1, 0)])
    id_tile = held // 2 * (enc // LANES)
    all_ids = own[:, id_tile, 0, :ref_count].astype(jnp.int32).reshape(-1)
    windows = jnp.concatenate([all_ids[:2], all_ids[:-2]])

    live = (seq_index > 0).astype(jnp.int32).reshape(1)
    packed = [
        pack(core, windows, own, other, enc, c * chunk_groups, group_count, chunk_groups)
        for c in range(CHUNKS)
    ]
    rows = [exchange(p, SEQ) for p in packed]

    z_index = lax.axis_index("z")
    column = lax.dynamic_index_in_dim(
        windows.reshape(x_count, z_count, ref_count), z_index, axis=1, keepdims=False
    )
    column_live = (
        (jnp.arange(x_count)[:, None] > 0) | (z_index > 0) | (jnp.arange(ref_count)[None, :] >= 2)
    )
    column = jnp.where(column_live, column, -1)
    column, _ = lax.optimization_barrier((column, packed[-1]))
    line_ids = lax.all_gather(column, "y", axis=0, tiled=False).reshape(line, group_count, 1, 2, 1)
    slots = seq_count * held * own_tokens
    other_core = (jnp.arange(2) != core)[None, None, :, None, None]
    keys = jnp.where(
        line_ids >= 0, other_core * slots + line_ids * own_tokens + jnp.arange(own_tokens), -1
    )
    matches = [
        (
            jnp.arange(2 * slots)[:, None]
            == keys[:, c * chunk_groups : (c + 1) * chunk_groups].reshape(1, -1)
        ).astype(BF16)
        for c in range(CHUNKS)
    ]
    live, matches = lax.optimization_barrier((live, matches))

    done = ()
    total = jnp.zeros((2 * slots, enc), F32)
    for c in range(CHUNKS):
        *done, terms = attend(
            live, rows[c], kv_weight, queries[0], out_grad[0], done, c * chunk_groups, line
        )
        back = exchange(terms, LINE)
        total = total + jnp.dot(matches[c], back.reshape(-1, enc), preferred_element_type=F32)
    given = lax.ppermute(total[slots:].astype(BF16), "c", [(0, 1), (1, 0)])
    total = total[:slots] + given
    owned = exchange(total.astype(BF16).reshape(seq_count, held * own_tokens, enc), SEQ)
    owned = owned.reshape(x_count, z_count, held, own_tokens, enc).astype(F32).sum(axis=1)
    row_grad = owned.transpose(1, 0, 2, 3).reshape(held, x_count * own_tokens, enc)
    return done[0][None], done[1][None], row_grad


def solution(mesh):
    split = Mesh(mesh.devices.reshape(4, 2, 4, 4), ("y", "c", "x", "z"))
    return jax.shard_map(
        body,
        mesh=split,
        in_specs=(
            P(DP, SEQ, None),
            P(SEQ, None, None),
            P(),
            P(DP, SEQ, None),
            P(DP, SEQ, None),
        ),
        out_specs=(P(DP, SEQ, None), P(DP, SEQ, None), P(SEQ, DP, None)),
        check_vma=False,
    )
```

```python
import functools

import jax
import jax.numpy as jnp
from jax import lax
from jax.experimental import pallas as pl
from jax.experimental.pallas import tpu as pltpu
from jax.sharding import Mesh
from jax.sharding import PartitionSpec as P

HD = 128
GROUP = 64
SEQ = ("x", "z")
DP = ("y", "c")
LINE = ("y", "c", "x")
CHUNKS = 2
HEAD_BATCH = 8
LANES = 128
F32 = jnp.float32
BF16 = jnp.bfloat16


def dot(a, b, ca, cb):
    return lax.dot_general(a, b, (((ca,), (cb,)), ((), ())), preferred_element_type=F32)


def spread_kernel(core_ref, ids_ref, rows_ref, out_ref):
    half, tokens, enc = rows_ref.shape
    lane_tiles = enc // LANES
    lanes = lax.broadcasted_iota(jnp.int32, (8, LANES), 1)
    ids = jnp.zeros((8, LANES), jnp.int32)
    for g in range(ids_ref.shape[1]):
        for r in range(2):
            ids = jnp.where(lanes == 2 * g + r, ids_ref[r, g], ids)
    ids = ids.astype(F32).astype(BF16)
    for pair in range(tokens // 16):
        for j in range(half):
            for t in range(lane_tiles):
                rows = rows_ref[j, 16 * pair : 16 * pair + 16, t * LANES : (t + 1) * LANES].astype(F32)
                out_ref[2 * pair, j * lane_tiles + t] = rows[:8].astype(BF16)
                out_ref[2 * pair + 1, j * lane_tiles + t] = rows[8:].astype(BF16)
        out_ref[2 * pair, half * lane_tiles] = ids
        out_ref[2 * pair + 1, half * lane_tiles] = ids


def spread(core, ids, database, dests):
    held, tokens, enc = database.shape
    half = held // 2
    out = (dests, half * (enc // LANES) + 1, tokens // dests, LANES)
    return pl.pallas_call(
        spread_kernel,
        out_shape=pltpu.HBM(out, BF16),
        grid_spec=pltpu.PrefetchScalarGridSpec(
            num_scalar_prefetch=2,
            grid=(1,),
            in_specs=[pl.BlockSpec((half, tokens, enc), lambda i, core, ids: (core[0], 0, 0))],
            out_specs=pl.BlockSpec(out, lambda i, core, ids: (0, 0, 0, 0)),
        ),
        compiler_params=pltpu.CompilerParams(vmem_limit_bytes=16 << 20),
        name="spread",
    )(core, *in_hbm(ids, database))


def pack_kernel(
    first_group, group_count, chunk_groups, lane_tiles, core_ref, ids_ref, own_ref, other_ref, out_ref
):
    def load(ref_id, t):
        at = (ref_id >> 2, (ref_id & 1) * lane_tiles + t)
        own = ((ref_id >> 1) & 1) == core_ref[0]
        return jnp.where(own, own_ref[at].astype(F32), other_ref[at].astype(F32))

    def per_dest(dest, carry):
        for g in range(chunk_groups):
            at = dest * 2 * group_count + 2 * (first_group + g)
            first, second = ids_ref[at], ids_ref[at + 1]
            for t in range(lane_tiles):
                a, b = load(first, t), load(second, t)
                out_ref[dest, g, :, t * LANES : (t + 1) * LANES] = jnp.concatenate(
                    [a[:4], b[:4], a[4:], b[4:]], axis=0
                ).astype(BF16)
        return carry

    lax.fori_loop(0, out_ref.shape[0], per_dest, 0)


def pack(core, ids, own, other, enc, first_group, group_count, chunk_groups):
    dests = own.shape[0]
    return pl.pallas_call(
        functools.partial(pack_kernel, first_group, group_count, chunk_groups, enc // LANES),
        out_shape=jax.ShapeDtypeStruct((dests, chunk_groups, 16, enc), BF16),
        in_specs=[
            pl.BlockSpec(memory_space=pltpu.SMEM),
            pl.BlockSpec(memory_space=pltpu.SMEM),
            pl.BlockSpec(memory_space=pltpu.VMEM),
            pl.BlockSpec(memory_space=pltpu.VMEM),
        ],
        out_specs=pl.BlockSpec(memory_space=pltpu.VMEM),
        compiler_params=pltpu.CompilerParams(vmem_limit_bytes=16 << 20),
        name="pack",
    )(core, ids, own, other)


def attend_kernel(heads, first_group, live_ref, rows_ref, w_ref, q_ref, g_ref, *rest):
    att_ref, qg_ref, term_ref, kv, kv_grad, q_pair, g_pair, q_turned, g_turned = rest[-9:]
    scale = HD**-0.5
    width = heads * HD
    span = HEAD_BATCH * HD
    step = pl.program_id(0)
    live = (live_ref[0] > 0) | (step + first_group > 0)

    @pl.when(step == 0)
    def _():
        for ref in (q_pair, g_pair, q_turned, g_turned):
            ref[...] = jnp.zeros(ref.shape, BF16)

    queries = q_ref[...]
    grads = jnp.where(live, g_ref[...], jnp.zeros((), BF16))
    turned = jnp.transpose(queries), jnp.transpose(grads)
    for h in range(heads):
        c = slice(h * HD, (h + 1) * HD)
        r = slice(h * GROUP, (h + 1) * GROUP)
        in_pair = slice(h % 2 * HD, (h % 2 + 1) * HD)
        in_four = slice(h % 4 * GROUP, (h % 4 + 1) * GROUP)
        q_pair[r, in_pair] = queries[:, c]
        g_pair[r, in_pair] = grads[:, c]
        q_turned[c, in_four] = turned[0][c]
        g_turned[c, in_four] = turned[1][c]

    def project(base):
        rows = rows_ref[:, step].reshape(-1, rows_ref.shape[-1])
        for start in (base * HD, width + base * HD):
            part = slice(start, start + span)
            kv[:, part] = dot(rows, w_ref[:, part], 1, 0).astype(BF16)

    project(0)
    for base in range(0, heads, HEAD_BATCH):
        pairs = range(base // 2, (base + HEAD_BATCH) // 2)
        keys = [slice(p * 2 * HD, (p + 1) * 2 * HD) for p in pairs]
        values = [slice(width + p * 2 * HD, width + (p + 1) * 2 * HD) for p in pairs]
        rows_of = [slice(p * 2 * GROUP, (p + 1) * 2 * GROUP) for p in pairs]
        scores = [dot(q_pair[r], kv[:, k], 1, 1) * scale for r, k in zip(rows_of, keys)]
        grad_probs = [dot(g_pair[r], kv[:, v], 1, 1) for r, v in zip(rows_of, values)]
        if base + HEAD_BATCH < heads:
            project(base + HEAD_BATCH)
        raised = [jnp.exp(s - jnp.max(s, axis=-1, keepdims=True)) for s in scores]
        probs = [e / jnp.sum(e, axis=-1, keepdims=True) for e in raised]
        halves = [p.astype(BF16) for p in probs]
        score_grads = [
            (p * (gp - jnp.sum(p * gp, axis=-1, keepdims=True))).astype(BF16)
            for p, gp in zip(probs, grad_probs)
        ]
        for p, k, v, half, sg in zip(pairs, keys, values, halves, score_grads):
            attended = dot(half, kv[:, v], 1, 0)
            query_grad = dot(sg, kv[:, k], 1, 0)
            for i in range(2):
                c = slice((2 * p + i) * HD, (2 * p + i + 1) * HD)
                at = slice(i * GROUP, (i + 1) * GROUP), slice(i * HD, (i + 1) * HD)
                att_ref[:, c] = jnp.where(live, attended[at], 0.0).astype(BF16)
                qg_ref[:, c] = (query_grad[at] * scale).astype(BF16)
        for i in range(0, len(pairs), 2):
            k = slice(keys[i].start, keys[i + 1].stop)
            v = slice(values[i].start, values[i + 1].stop)
            sg = jnp.concatenate(score_grads[i : i + 2], axis=0)
            half = jnp.concatenate(halves[i : i + 2], axis=0)
            kv_grad[k, :] = (dot(q_turned[k, :], sg, 1, 0) * scale).astype(BF16)
            kv_grad[v, :] = dot(g_turned[k, :], half, 1, 0).astype(BF16)
    terms = jnp.transpose(dot(w_ref[...], kv_grad[...], 1, 0)).astype(BF16)
    term_ref[...] = terms.reshape(term_ref.shape)


def in_hbm(*arrays):
    return [pltpu.with_memory_space_constraint(a, pltpu.HBM) for a in arrays]


def attend(live, rows, weight, queries, grads, before, first_group, line):
    slices, chunk_groups, _, enc = rows.shape
    tokens, width = queries.shape
    keys = slices * 16
    block = pl.BlockSpec((GROUP, width), lambda i, l: (i + first_group, 0))
    flops = chunk_groups * (2 * 2 * keys * enc * 2 * width + 6 * 2 * GROUP * keys * width)
    return pl.pallas_call(
        functools.partial(attend_kernel, width // HD, first_group),
        out_shape=[
            pltpu.HBM((tokens, width), BF16),
            pltpu.HBM((tokens, width), BF16),
            pltpu.HBM((line, chunk_groups, keys // line, enc), BF16),
        ],
        grid_spec=pltpu.PrefetchScalarGridSpec(
            num_scalar_prefetch=1,
            grid=(chunk_groups,),
            in_specs=[
                pl.BlockSpec(memory_space=pltpu.VMEM),
                pl.BlockSpec(weight.shape, lambda i, l: (0, 0), pipeline_mode=pl.Buffered(1)),
                block,
                block,
            ]
            + [pl.BlockSpec(memory_space=pl.ANY)] * len(before),
            out_specs=[
                block,
                block,
                pl.BlockSpec((line, 1, keys // line, enc), lambda i, l: (0, i, 0, 0)),
            ],
            scratch_shapes=[
                pltpu.VMEM((keys, 2 * width), BF16),
                pltpu.VMEM((2 * width, keys), BF16),
                pltpu.VMEM((width // 2, 2 * HD), BF16),
                pltpu.VMEM((width // 2, 2 * HD), BF16),
                pltpu.VMEM((width, 4 * GROUP), BF16),
                pltpu.VMEM((width, 4 * GROUP), BF16),
            ],
        ),
        input_output_aliases={5 + n: n for n in range(len(before))},
        cost_estimate=pl.CostEstimate(flops=flops, bytes_accessed=16 << 20, transcendentals=0),
        compiler_params=pltpu.CompilerParams(vmem_limit_bytes=32 << 20),
        name="attend",
    )(live, rows, *in_hbm(weight, queries, grads, *before))


def exchange(block, axes):
    return lax.all_to_all(block, axes, split_axis=0, concat_axis=0, tiled=True)


def body(queries, database, kv_weight, neighbours, out_grad):
    seq_count = lax.axis_size(SEQ)
    seq_index = lax.axis_index(SEQ)
    x_count, z_count = lax.axis_size("x"), lax.axis_size("z")
    dp_count = lax.axis_size(DP)
    line = lax.axis_size(LINE)
    group_count = neighbours.shape[1]
    ref_count = 2 * group_count
    held, row_tokens, enc = database.shape
    width = queries.shape[2]
    chunk_groups = group_count // CHUNKS
    own_tokens = row_tokens // line

    core = lax.axis_index("c").astype(jnp.int32).reshape(1)
    own = exchange(spread(core, neighbours[0].T, database, seq_count), SEQ)
    other = lax.ppermute(own, "c", [(0, 1), (1, 0)])
    id_tile = held // 2 * (enc // LANES)
    all_ids = own[:, id_tile, 0, :ref_count].astype(jnp.int32).reshape(-1)
    windows = jnp.concatenate([all_ids[:2], all_ids[:-2]])

    live = (seq_index > 0).astype(jnp.int32).reshape(1)
    packed = [
        pack(core, windows, own, other, enc, c * chunk_groups, group_count, chunk_groups)
        for c in range(CHUNKS)
    ]
    rows = [exchange(p, SEQ) for p in packed]

    z_index = lax.axis_index("z")
    column = lax.dynamic_index_in_dim(
        windows.reshape(x_count, z_count, ref_count), z_index, axis=1, keepdims=False
    )
    column_live = (
        (jnp.arange(x_count)[:, None] > 0) | (z_index > 0) | (jnp.arange(ref_count)[None, :] >= 2)
    )
    column = jnp.where(column_live, column, -1)
    column, _ = lax.optimization_barrier((column, packed[-1]))
    line_ids = lax.all_gather(column, DP, axis=0, tiled=False).reshape(line, group_count, 2)
    keys = jnp.where(
        line_ids[..., None] >= 0, line_ids[..., None] * own_tokens + jnp.arange(own_tokens), -1
    )

    slots = seq_count * held * own_tokens
    matches = [
        (
            jnp.arange(slots)[:, None]
            == keys[:, c * chunk_groups : (c + 1) * chunk_groups].reshape(1, -1)
        ).astype(BF16)
        for c in range(CHUNKS)
    ]
    live, matches = lax.optimization_barrier((live, matches))

    done = ()
    total = jnp.zeros((slots, enc), F32)
    for c in range(CHUNKS):
        *done, terms = attend(
            live, rows[c], kv_weight, queries[0], out_grad[0], done, c * chunk_groups, line
        )
        back = exchange(terms, LINE)
        total = total + jnp.dot(matches[c], back.reshape(-1, enc), preferred_element_type=F32)
    owned = exchange(total.astype(BF16).reshape(seq_count, held * own_tokens, enc), SEQ)
    owned = owned.reshape(x_count, z_count, held, own_tokens, enc).astype(F32).sum(axis=1)
    row_grad = owned.transpose(1, 0, 2, 3).reshape(held, x_count * own_tokens, enc)
    return done[0][None], done[1][None], row_grad


def solution(mesh):
    split = Mesh(mesh.devices.reshape(4, 2, 4, 4), ("y", "c", "x", "z"))
    return jax.shard_map(
        body,
        mesh=split,
        in_specs=(
            P(DP, SEQ, None),
            P(SEQ, None, None),
            P(),
            P(DP, SEQ, None),
            P(DP, SEQ, None),
        ),
        out_specs=(P(DP, SEQ, None), P(DP, SEQ, None), P(SEQ, DP, None)),
        check_vma=False,
    )
```

```python
import functools

import jax
import jax.numpy as jnp
from jax import lax
from jax.experimental import pallas as pl
from jax.experimental.pallas import tpu as pltpu
from jax.sharding import Mesh
from jax.sharding import PartitionSpec as P

HD = 128
GROUP = 64
SEQ = ("x", "z")
DP = ("y", "c")
LINE = ("y", "c", "x")
CHUNKS = 2
HEAD_BATCH = 8
LANES = 128
F32 = jnp.float32
BF16 = jnp.bfloat16


def dot(a, b, ca, cb):
    return lax.dot_general(a, b, (((ca,), (cb,)), ((), ())), preferred_element_type=F32)


def spread_kernel(core_ref, ids_ref, rows_ref, out_ref):
    half, tokens, enc = rows_ref.shape
    lane_tiles = enc // LANES
    lanes = lax.broadcasted_iota(jnp.int32, (8, LANES), 1)
    ids = jnp.zeros((8, LANES), jnp.int32)
    for g in range(ids_ref.shape[1]):
        for r in range(2):
            ids = jnp.where(lanes == 2 * g + r, ids_ref[r, g], ids)
    ids = ids.astype(F32).astype(BF16)
    for pair in range(tokens // 16):
        for j in range(half):
            for t in range(lane_tiles):
                rows = rows_ref[j, 16 * pair : 16 * pair + 16, t * LANES : (t + 1) * LANES].astype(F32)
                out_ref[2 * pair, j * lane_tiles + t] = rows[:8].astype(BF16)
                out_ref[2 * pair + 1, j * lane_tiles + t] = rows[8:].astype(BF16)
        out_ref[2 * pair, half * lane_tiles] = ids
        out_ref[2 * pair + 1, half * lane_tiles] = ids


def spread(core, ids, database, dests):
    held, tokens, enc = database.shape
    half = held // 2
    out = (dests, half * (enc // LANES) + 1, tokens // dests, LANES)
    return pl.pallas_call(
        spread_kernel,
        out_shape=jax.ShapeDtypeStruct(out, BF16),
        grid_spec=pltpu.PrefetchScalarGridSpec(
            num_scalar_prefetch=2,
            grid=(1,),
            in_specs=[pl.BlockSpec((half, tokens, enc), lambda i, core, ids: (core[0], 0, 0))],
            out_specs=pl.BlockSpec(out, lambda i, core, ids: (0, 0, 0, 0)),
        ),
        compiler_params=pltpu.CompilerParams(vmem_limit_bytes=16 << 20),
        name="spread",
    )(core, *in_hbm(ids, database))


def pack_kernel(
    first_group, group_count, chunk_groups, lane_tiles, core_ref, ids_ref, own_ref, other_ref, out_ref
):
    def load(ref_id, t):
        at = (ref_id >> 2, (ref_id & 1) * lane_tiles + t)
        own = ((ref_id >> 1) & 1) == core_ref[0]
        return jnp.where(own, own_ref[at].astype(F32), other_ref[at].astype(F32))

    def per_dest(dest, carry):
        for g in range(chunk_groups):
            at = dest * 2 * group_count + 2 * (first_group + g)
            first, second = ids_ref[at], ids_ref[at + 1]
            for t in range(lane_tiles):
                a, b = load(first, t), load(second, t)
                out_ref[dest, g, :, t * LANES : (t + 1) * LANES] = jnp.concatenate(
                    [a[:4], b[:4], a[4:], b[4:]], axis=0
                ).astype(BF16)
        return carry

    lax.fori_loop(0, out_ref.shape[0], per_dest, 0, unroll=2)


def pack(core, ids, own, other, enc, first_group, group_count, chunk_groups):
    dests = own.shape[0]
    return pl.pallas_call(
        functools.partial(pack_kernel, first_group, group_count, chunk_groups, enc // LANES),
        out_shape=jax.ShapeDtypeStruct((dests, chunk_groups, 16, enc), BF16),
        in_specs=[
            pl.BlockSpec(memory_space=pltpu.SMEM),
            pl.BlockSpec(memory_space=pltpu.SMEM),
            pl.BlockSpec(memory_space=pltpu.VMEM),
            pl.BlockSpec(memory_space=pltpu.VMEM),
        ],
        out_specs=pl.BlockSpec(memory_space=pltpu.VMEM),
        compiler_params=pltpu.CompilerParams(vmem_limit_bytes=16 << 20),
        name="pack",
    )(core, ids, own, other)


def attend_kernel(heads, first_group, live_ref, rows_ref, w_ref, q_ref, g_ref, *rest):
    att_ref, qg_ref, term_ref, kv, kv_grad, q_pair, g_pair, q_turned, g_turned = rest[-9:]
    scale = HD**-0.5
    width = heads * HD
    span = HEAD_BATCH * HD
    step = pl.program_id(0)
    live = (live_ref[0] > 0) | (step + first_group > 0)

    @pl.when(step == 0)
    def _():
        for ref in (q_pair, g_pair, q_turned, g_turned):
            ref[...] = jnp.zeros(ref.shape, BF16)

    queries = q_ref[...]
    grads = jnp.where(live, g_ref[...], jnp.zeros((), BF16))
    turned = jnp.transpose(queries), jnp.transpose(grads)
    for h in range(heads):
        c = slice(h * HD, (h + 1) * HD)
        r = slice(h * GROUP, (h + 1) * GROUP)
        in_pair = slice(h % 2 * HD, (h % 2 + 1) * HD)
        in_four = slice(h % 4 * GROUP, (h % 4 + 1) * GROUP)
        q_pair[r, in_pair] = queries[:, c]
        g_pair[r, in_pair] = grads[:, c]
        q_turned[c, in_four] = turned[0][c]
        g_turned[c, in_four] = turned[1][c]

    def project(base):
        rows = rows_ref[:, step].reshape(-1, rows_ref.shape[-1])
        for start in (base * HD, width + base * HD):
            part = slice(start, start + span)
            kv[:, part] = dot(rows, w_ref[:, part], 1, 0).astype(BF16)

    project(0)
    for base in range(0, heads, HEAD_BATCH):
        pairs = range(base // 2, (base + HEAD_BATCH) // 2)
        keys = [slice(p * 2 * HD, (p + 1) * 2 * HD) for p in pairs]
        values = [slice(width + p * 2 * HD, width + (p + 1) * 2 * HD) for p in pairs]
        rows_of = [slice(p * 2 * GROUP, (p + 1) * 2 * GROUP) for p in pairs]
        scores = [dot(q_pair[r], kv[:, k], 1, 1) * scale for r, k in zip(rows_of, keys)]
        grad_probs = [dot(g_pair[r], kv[:, v], 1, 1) for r, v in zip(rows_of, values)]
        if base + HEAD_BATCH < heads:
            project(base + HEAD_BATCH)
        raised = [jnp.exp(s - jnp.max(s, axis=-1, keepdims=True)) for s in scores]
        probs = [e / jnp.sum(e, axis=-1, keepdims=True) for e in raised]
        halves = [p.astype(BF16) for p in probs]
        score_grads = [
            (p * (gp - jnp.sum(p * gp, axis=-1, keepdims=True))).astype(BF16)
            for p, gp in zip(probs, grad_probs)
        ]
        for p, k, v, half, sg in zip(pairs, keys, values, halves, score_grads):
            attended = dot(half, kv[:, v], 1, 0)
            query_grad = dot(sg, kv[:, k], 1, 0)
            for i in range(2):
                c = slice((2 * p + i) * HD, (2 * p + i + 1) * HD)
                at = slice(i * GROUP, (i + 1) * GROUP), slice(i * HD, (i + 1) * HD)
                att_ref[:, c] = jnp.where(live, attended[at], 0.0).astype(BF16)
                qg_ref[:, c] = (query_grad[at] * scale).astype(BF16)
        for i in range(0, len(pairs), 2):
            k = slice(keys[i].start, keys[i + 1].stop)
            v = slice(values[i].start, values[i + 1].stop)
            sg = jnp.concatenate(score_grads[i : i + 2], axis=0)
            half = jnp.concatenate(halves[i : i + 2], axis=0)
            kv_grad[k, :] = (dot(q_turned[k, :], sg, 1, 0) * scale).astype(BF16)
            kv_grad[v, :] = dot(g_turned[k, :], half, 1, 0).astype(BF16)
    terms = jnp.transpose(dot(w_ref[...], kv_grad[...], 1, 0)).astype(BF16)
    term_ref[...] = terms.reshape(term_ref.shape)


def in_hbm(*arrays):
    return [pltpu.with_memory_space_constraint(a, pltpu.HBM) for a in arrays]


def attend(live, rows, weight, queries, grads, before, first_group, line):
    slices, chunk_groups, _, enc = rows.shape
    tokens, width = queries.shape
    keys = slices * 16
    block = pl.BlockSpec((GROUP, width), lambda i, l: (i + first_group, 0))
    flops = chunk_groups * (2 * 2 * keys * enc * 2 * width + 6 * 2 * GROUP * keys * width)
    return pl.pallas_call(
        functools.partial(attend_kernel, width // HD, first_group),
        out_shape=[
            pltpu.HBM((tokens, width), BF16),
            pltpu.HBM((tokens, width), BF16),
            pltpu.HBM((line, chunk_groups, keys // line, enc), BF16),
        ],
        grid_spec=pltpu.PrefetchScalarGridSpec(
            num_scalar_prefetch=1,
            grid=(chunk_groups,),
            in_specs=[
                pl.BlockSpec(memory_space=pltpu.VMEM),
                pl.BlockSpec(weight.shape, lambda i, l: (0, 0), pipeline_mode=pl.Buffered(1)),
                block,
                block,
            ]
            + [pl.BlockSpec(memory_space=pl.ANY)] * len(before),
            out_specs=[
                block,
                block,
                pl.BlockSpec((line, 1, keys // line, enc), lambda i, l: (0, i, 0, 0)),
            ],
            scratch_shapes=[
                pltpu.VMEM((keys, 2 * width), BF16),
                pltpu.VMEM((2 * width, keys), BF16),
                pltpu.VMEM((width // 2, 2 * HD), BF16),
                pltpu.VMEM((width // 2, 2 * HD), BF16),
                pltpu.VMEM((width, 4 * GROUP), BF16),
                pltpu.VMEM((width, 4 * GROUP), BF16),
            ],
        ),
        input_output_aliases={5 + n: n for n in range(len(before))},
        cost_estimate=pl.CostEstimate(flops=flops, bytes_accessed=16 << 20, transcendentals=0),
        compiler_params=pltpu.CompilerParams(vmem_limit_bytes=32 << 20),
        name="attend",
    )(live, rows, *in_hbm(weight, queries, grads, *before))


def collect_kernel(x_count, pieces_ref, out_ref):
    z_count = pieces_ref.shape[0] // x_count
    held = out_ref.shape[0]
    own = pieces_ref.shape[1] // held
    sums = []
    for x in range(x_count):
        total = pieces_ref[x * z_count].astype(F32)
        for z in range(1, z_count):
            total = total + pieces_ref[x * z_count + z].astype(F32)
        sums.append(total)
    for n in range(held):
        out_ref[n] = jnp.concatenate([t[n * own : (n + 1) * own] for t in sums], axis=0)


def collect(pieces, x_count, held):
    enc = pieces.shape[2]
    return pl.pallas_call(
        functools.partial(collect_kernel, x_count),
        out_shape=jax.ShapeDtypeStruct((held, x_count * pieces.shape[1] // held, enc), F32),
        in_specs=[pl.BlockSpec(memory_space=pltpu.VMEM)],
        out_specs=pl.BlockSpec(memory_space=pltpu.VMEM),
        compiler_params=pltpu.CompilerParams(vmem_limit_bytes=16 << 20),
        name="collect",
    )(pieces)


def exchange(block, axes):
    return lax.all_to_all(block, axes, split_axis=0, concat_axis=0, tiled=True)


def body(queries, database, kv_weight, neighbours, out_grad):
    seq_count = lax.axis_size(SEQ)
    seq_index = lax.axis_index(SEQ)
    x_count, z_count = lax.axis_size("x"), lax.axis_size("z")
    dp_count = lax.axis_size(DP)
    line = lax.axis_size(LINE)
    group_count = neighbours.shape[1]
    ref_count = 2 * group_count
    held, row_tokens, enc = database.shape
    width = queries.shape[2]
    chunk_groups = group_count // CHUNKS
    own_tokens = row_tokens // line

    core = lax.axis_index("c").astype(jnp.int32).reshape(1)
    own = exchange(spread(core, neighbours[0].T, database, seq_count), SEQ)
    other = lax.ppermute(own, "c", [(0, 1), (1, 0)])
    id_tile = held // 2 * (enc // LANES)
    all_ids = own[:, id_tile, 0, :ref_count].astype(jnp.int32).reshape(-1)
    windows = jnp.concatenate([all_ids[:2], all_ids[:-2]])

    live = (seq_index > 0).astype(jnp.int32).reshape(1)
    packed = [
        pack(core, windows, own, other, enc, c * chunk_groups, group_count, chunk_groups)
        for c in range(CHUNKS)
    ]
    rows = [exchange(p, SEQ) for p in packed]

    z_index = lax.axis_index("z")
    column = lax.dynamic_index_in_dim(
        windows.reshape(x_count, z_count, ref_count), z_index, axis=1, keepdims=False
    )
    column_live = (
        (jnp.arange(x_count)[:, None] > 0) | (z_index > 0) | (jnp.arange(ref_count)[None, :] >= 2)
    )
    column = jnp.where(column_live, column, -1)
    column, _ = lax.optimization_barrier((column, packed[-1]))
    line_ids = lax.all_gather(column, DP, axis=0, tiled=False).reshape(line, group_count, 2)
    keys = jnp.where(
        line_ids[..., None] >= 0, line_ids[..., None] * own_tokens + jnp.arange(own_tokens), -1
    )

    slots = seq_count * held * own_tokens
    matches = [
        (
            jnp.arange(slots)[:, None]
            == keys[:, c * chunk_groups : (c + 1) * chunk_groups].reshape(1, -1)
        ).astype(BF16)
        for c in range(CHUNKS)
    ]
    live, matches = lax.optimization_barrier((live, matches))

    done = ()
    total = jnp.zeros((slots, enc), F32)
    for c in range(CHUNKS):
        *done, terms = attend(
            live, rows[c], kv_weight, queries[0], out_grad[0], done, c * chunk_groups, line
        )
        back = exchange(terms, LINE)
        total = total + jnp.dot(matches[c], back.reshape(-1, enc), preferred_element_type=F32)
    owned = exchange(total.astype(BF16).reshape(seq_count, held * own_tokens, enc), SEQ)
    row_grad = collect(owned, x_count, held)
    return done[0][None], done[1][None], row_grad


def solution(mesh):
    split = Mesh(mesh.devices.reshape(4, 2, 4, 4), ("y", "c", "x", "z"))
    return jax.shard_map(
        body,
        mesh=split,
        in_specs=(
            P(DP, SEQ, None),
            P(SEQ, None, None),
            P(),
            P(DP, SEQ, None),
            P(DP, SEQ, None),
        ),
        out_specs=(P(DP, SEQ, None), P(DP, SEQ, None), P(SEQ, DP, None)),
        check_vma=False,
    )
```

```python
import functools

import jax
import jax.numpy as jnp
from jax import lax
from jax.experimental import pallas as pl
from jax.experimental.pallas import tpu as pltpu
from jax.sharding import Mesh
from jax.sharding import PartitionSpec as P

HD = 128
GROUP = 64
SEQ = ("x", "z")
DP = ("y", "c")
LINE = ("y", "c", "x")
CHUNKS = 2
HEAD_BATCH = 8
LANES = 128
PACK_STEPS = 4
F32 = jnp.float32
BF16 = jnp.bfloat16


def dot(a, b, ca, cb):
    return lax.dot_general(a, b, (((ca,), (cb,)), ((), ())), preferred_element_type=F32)


def spread_kernel(core_ref, ids_ref, rows_ref, out_ref):
    half, tokens, enc = rows_ref.shape
    lane_tiles = enc // LANES
    lanes = lax.broadcasted_iota(jnp.int32, (8, LANES), 1)
    ids = jnp.zeros((8, LANES), jnp.int32)
    for g in range(ids_ref.shape[1]):
        for r in range(2):
            ids = jnp.where(lanes == 2 * g + r, ids_ref[r, g], ids)
    ids = ids.astype(F32).astype(BF16)
    for pair in range(tokens // 16):
        for j in range(half):
            for t in range(lane_tiles):
                rows = rows_ref[j, 16 * pair : 16 * pair + 16, t * LANES : (t + 1) * LANES].astype(F32)
                out_ref[2 * pair, j * lane_tiles + t] = rows[:8].astype(BF16)
                out_ref[2 * pair + 1, j * lane_tiles + t] = rows[8:].astype(BF16)
        out_ref[2 * pair, half * lane_tiles] = ids
        out_ref[2 * pair + 1, half * lane_tiles] = ids


def spread(core, ids, database, dests):
    held, tokens, enc = database.shape
    half = held // 2
    out = (dests, half * (enc // LANES) + 1, tokens // dests, LANES)
    return pl.pallas_call(
        spread_kernel,
        out_shape=jax.ShapeDtypeStruct(out, BF16),
        grid_spec=pltpu.PrefetchScalarGridSpec(
            num_scalar_prefetch=2,
            grid=(1,),
            in_specs=[pl.BlockSpec((half, tokens, enc), lambda i, core, ids: (core[0], 0, 0))],
            out_specs=pl.BlockSpec(out, lambda i, core, ids: (0, 0, 0, 0)),
        ),
        compiler_params=pltpu.CompilerParams(vmem_limit_bytes=16 << 20),
        name="spread",
    )(core, *in_hbm(ids, database))


def pack_kernel(
    first_group, group_count, chunk_groups, lane_tiles, core_ref, ids_ref, own_ref, other_ref, out_ref
):
    step = pl.program_id(0)

    def load(ref_id, t):
        at = (ref_id >> 2, (ref_id & 1) * lane_tiles + t)
        own = ((ref_id >> 1) & 1) == core_ref[0]
        return jnp.where(own, own_ref[at].astype(F32), other_ref[at].astype(F32))

    def per_dest(dest, carry):
        for g in range(chunk_groups):
            at = (step * out_ref.shape[0] + dest) * 2 * group_count + 2 * (first_group + g)
            first, second = ids_ref[at], ids_ref[at + 1]
            for t in range(lane_tiles):
                a, b = load(first, t), load(second, t)
                out_ref[dest, g, :, t * LANES : (t + 1) * LANES] = jnp.concatenate(
                    [a[:4], b[:4], a[4:], b[4:]], axis=0
                ).astype(BF16)
        return carry

    lax.fori_loop(0, out_ref.shape[0], per_dest, 0, unroll=2)


def pack(core, ids, own, other, enc, first_group, group_count, chunk_groups):
    dests = own.shape[0]
    return pl.pallas_call(
        functools.partial(pack_kernel, first_group, group_count, chunk_groups, enc // LANES),
        out_shape=jax.ShapeDtypeStruct((dests, chunk_groups, 16, enc), BF16),
        in_specs=[
            pl.BlockSpec(memory_space=pltpu.SMEM),
            pl.BlockSpec(memory_space=pltpu.SMEM),
            pl.BlockSpec(memory_space=pltpu.VMEM),
            pl.BlockSpec(memory_space=pltpu.VMEM),
        ],
        grid=(PACK_STEPS,),
        out_specs=pl.BlockSpec(
            (dests // PACK_STEPS, chunk_groups, 16, enc), lambda i: (i, 0, 0, 0)
        ),
        compiler_params=pltpu.CompilerParams(vmem_limit_bytes=16 << 20),
        name="pack",
    )(core, ids, own, other)


def attend_kernel(heads, first_group, live_ref, rows_ref, w_ref, q_ref, g_ref, *rest):
    att_ref, qg_ref, term_ref, kv, kv_grad, q_pair, g_pair, q_turned, g_turned = rest[-9:]
    scale = HD**-0.5
    width = heads * HD
    span = HEAD_BATCH * HD
    step = pl.program_id(0)
    live = (live_ref[0] > 0) | (step + first_group > 0)

    @pl.when(step == 0)
    def _():
        for ref in (q_pair, g_pair, q_turned, g_turned):
            ref[...] = jnp.zeros(ref.shape, BF16)

    queries = q_ref[...]
    grads = jnp.where(live, g_ref[...], jnp.zeros((), BF16))
    turned = jnp.transpose(queries), jnp.transpose(grads)
    for h in range(heads):
        c = slice(h * HD, (h + 1) * HD)
        r = slice(h * GROUP, (h + 1) * GROUP)
        in_pair = slice(h % 2 * HD, (h % 2 + 1) * HD)
        in_four = slice(h % 4 * GROUP, (h % 4 + 1) * GROUP)
        q_pair[r, in_pair] = queries[:, c]
        g_pair[r, in_pair] = grads[:, c]
        q_turned[c, in_four] = turned[0][c]
        g_turned[c, in_four] = turned[1][c]

    def project(base):
        rows = rows_ref[:, step if first_group == 0 else 0].reshape(-1, rows_ref.shape[-1])
        for start in (base * HD, width + base * HD):
            part = slice(start, start + span)
            kv[:, part] = dot(rows, w_ref[:, part], 1, 0).astype(BF16)

    project(0)
    for base in range(0, heads, HEAD_BATCH):
        pairs = range(base // 2, (base + HEAD_BATCH) // 2)
        keys = [slice(p * 2 * HD, (p + 1) * 2 * HD) for p in pairs]
        values = [slice(width + p * 2 * HD, width + (p + 1) * 2 * HD) for p in pairs]
        rows_of = [slice(p * 2 * GROUP, (p + 1) * 2 * GROUP) for p in pairs]
        scores = [dot(q_pair[r], kv[:, k], 1, 1) * scale for r, k in zip(rows_of, keys)]
        grad_probs = [dot(g_pair[r], kv[:, v], 1, 1) for r, v in zip(rows_of, values)]
        if base + HEAD_BATCH < heads:
            project(base + HEAD_BATCH)
        raised = [jnp.exp(s - jnp.max(s, axis=-1, keepdims=True)) for s in scores]
        probs = [e / jnp.sum(e, axis=-1, keepdims=True) for e in raised]
        halves = [p.astype(BF16) for p in probs]
        score_grads = [
            (p * (gp - jnp.sum(p * gp, axis=-1, keepdims=True))).astype(BF16)
            for p, gp in zip(probs, grad_probs)
        ]
        for p, k, v, half, sg in zip(pairs, keys, values, halves, score_grads):
            attended = dot(half, kv[:, v], 1, 0)
            query_grad = dot(sg, kv[:, k], 1, 0)
            for i in range(2):
                c = slice((2 * p + i) * HD, (2 * p + i + 1) * HD)
                at = slice(i * GROUP, (i + 1) * GROUP), slice(i * HD, (i + 1) * HD)
                att_ref[:, c] = jnp.where(live, attended[at], 0.0).astype(BF16)
                qg_ref[:, c] = (query_grad[at] * scale).astype(BF16)
        for i in range(0, len(pairs), 2):
            k = slice(keys[i].start, keys[i + 1].stop)
            v = slice(values[i].start, values[i + 1].stop)
            sg = jnp.concatenate(score_grads[i : i + 2], axis=0)
            half = jnp.concatenate(halves[i : i + 2], axis=0)
            kv_grad[k, :] = (dot(q_turned[k, :], sg, 1, 0) * scale).astype(BF16)
            kv_grad[v, :] = dot(g_turned[k, :], half, 1, 0).astype(BF16)
    terms = jnp.transpose(dot(w_ref[...], kv_grad[...], 1, 0)).astype(BF16)
    term_ref[...] = terms.reshape(term_ref.shape)


def in_hbm(*arrays):
    return [pltpu.with_memory_space_constraint(a, pltpu.HBM) for a in arrays]


def attend(live, rows, weight, queries, grads, before, first_group, line):
    slices, chunk_groups, _, enc = rows.shape
    tokens, width = queries.shape
    keys = slices * 16
    block = pl.BlockSpec((GROUP, width), lambda i, l: (i + first_group, 0))
    flops = chunk_groups * (2 * 2 * keys * enc * 2 * width + 6 * 2 * GROUP * keys * width)
    return pl.pallas_call(
        functools.partial(attend_kernel, width // HD, first_group),
        out_shape=[
            pltpu.HBM((tokens, width), BF16),
            pltpu.HBM((tokens, width), BF16),
            pltpu.HBM((line, chunk_groups, keys // line, enc), BF16),
        ],
        grid_spec=pltpu.PrefetchScalarGridSpec(
            num_scalar_prefetch=1,
            grid=(chunk_groups,),
            in_specs=[
                pl.BlockSpec(memory_space=pltpu.VMEM)
                if first_group == 0
                else pl.BlockSpec((slices, 1, 16, enc), lambda i, l: (0, i, 0, 0)),
                pl.BlockSpec(weight.shape, lambda i, l: (0, 0), pipeline_mode=pl.Buffered(1)),
                block,
                block,
            ]
            + [pl.BlockSpec(memory_space=pl.ANY)] * len(before),
            out_specs=[
                block,
                block,
                pl.BlockSpec((line, 1, keys // line, enc), lambda i, l: (0, i, 0, 0)),
            ],
            scratch_shapes=[
                pltpu.VMEM((keys, 2 * width), BF16),
                pltpu.VMEM((2 * width, keys), BF16),
                pltpu.VMEM((width // 2, 2 * HD), BF16),
                pltpu.VMEM((width // 2, 2 * HD), BF16),
                pltpu.VMEM((width, 4 * GROUP), BF16),
                pltpu.VMEM((width, 4 * GROUP), BF16),
            ],
        ),
        input_output_aliases={5 + n: n for n in range(len(before))},
        cost_estimate=pl.CostEstimate(flops=flops, bytes_accessed=16 << 20, transcendentals=0),
        compiler_params=pltpu.CompilerParams(vmem_limit_bytes=32 << 20),
        name="attend",
    )(live, rows, *in_hbm(weight, queries, grads, *before))


def collect_kernel(x_count, pieces_ref, out_ref):
    z_count = pieces_ref.shape[0] // x_count
    held = out_ref.shape[0]
    own = pieces_ref.shape[1] // held
    sums = []
    for x in range(x_count):
        total = pieces_ref[x * z_count].astype(F32)
        for z in range(1, z_count):
            total = total + pieces_ref[x * z_count + z].astype(F32)
        sums.append(total)
    for n in range(held):
        out_ref[n] = jnp.concatenate([t[n * own : (n + 1) * own] for t in sums], axis=0)


def collect(pieces, x_count, held):
    enc = pieces.shape[2]
    return pl.pallas_call(
        functools.partial(collect_kernel, x_count),
        out_shape=jax.ShapeDtypeStruct((held, x_count * pieces.shape[1] // held, enc), F32),
        in_specs=[pl.BlockSpec(memory_space=pltpu.VMEM)],
        out_specs=pl.BlockSpec(memory_space=pltpu.VMEM),
        compiler_params=pltpu.CompilerParams(vmem_limit_bytes=16 << 20),
        name="collect",
    )(pieces)


def exchange(block, axes):
    return lax.all_to_all(block, axes, split_axis=0, concat_axis=0, tiled=True)


def body(queries, database, kv_weight, neighbours, out_grad):
    seq_count = lax.axis_size(SEQ)
    seq_index = lax.axis_index(SEQ)
    x_count, z_count = lax.axis_size("x"), lax.axis_size("z")
    dp_count = lax.axis_size(DP)
    line = lax.axis_size(LINE)
    group_count = neighbours.shape[1]
    ref_count = 2 * group_count
    held, row_tokens, enc = database.shape
    width = queries.shape[2]
    chunk_groups = group_count // CHUNKS
    own_tokens = row_tokens // line

    core = lax.axis_index("c").astype(jnp.int32).reshape(1)
    own = exchange(spread(core, neighbours[0].T, database, seq_count), SEQ)
    other = lax.ppermute(own, "c", [(0, 1), (1, 0)])
    id_tile = held // 2 * (enc // LANES)
    all_ids = own[:, id_tile, 0, :ref_count].astype(jnp.int32).reshape(-1)
    windows = jnp.concatenate([all_ids[:2], all_ids[:-2]])

    live = (seq_index > 0).astype(jnp.int32).reshape(1)
    packed = [
        pack(core, windows, own, other, enc, c * chunk_groups, group_count, chunk_groups)
        for c in range(CHUNKS)
    ]
    rows = [exchange(p, SEQ) for p in packed]

    z_index = lax.axis_index("z")
    column = lax.dynamic_index_in_dim(
        windows.reshape(x_count, z_count, ref_count), z_index, axis=1, keepdims=False
    )
    column_live = (
        (jnp.arange(x_count)[:, None] > 0) | (z_index > 0) | (jnp.arange(ref_count)[None, :] >= 2)
    )
    column = jnp.where(column_live, column, -1)
    column, _ = lax.optimization_barrier((column, packed[-1]))
    line_ids = lax.all_gather(column, DP, axis=0, tiled=False).reshape(line, group_count, 2)
    keys = jnp.where(
        line_ids[..., None] >= 0, line_ids[..., None] * own_tokens + jnp.arange(own_tokens), -1
    )

    slots = seq_count * held * own_tokens
    matches = [
        (
            jnp.arange(slots)[:, None]
            == keys[:, c * chunk_groups : (c + 1) * chunk_groups].reshape(1, -1)
        ).astype(BF16)
        for c in range(CHUNKS)
    ]
    live, matches = lax.optimization_barrier((live, matches))

    done = ()
    total = jnp.zeros((slots, enc), F32)
    for c in range(CHUNKS):
        *done, terms = attend(
            live, rows[c], kv_weight, queries[0], out_grad[0], done, c * chunk_groups, line
        )
        back = exchange(terms, LINE)
        total = total + jnp.dot(matches[c], back.reshape(-1, enc), preferred_element_type=F32)
    owned = exchange(total.astype(BF16).reshape(seq_count, held * own_tokens, enc), SEQ)
    row_grad = collect(owned, x_count, held)
    return done[0][None], done[1][None], row_grad


def solution(mesh):
    split = Mesh(mesh.devices.reshape(4, 2, 4, 4), ("y", "c", "x", "z"))
    return jax.shard_map(
        body,
        mesh=split,
        in_specs=(
            P(DP, SEQ, None),
            P(SEQ, None, None),
            P(),
            P(DP, SEQ, None),
            P(DP, SEQ, None),
        ),
        out_specs=(P(DP, SEQ, None), P(DP, SEQ, None), P(SEQ, DP, None)),
        check_vma=False,
    )
```
